32 devices in a mesh: ctx: 8 (over z, y), shard: 4 (over x, core).
Axes of the slice: x: 2, y: 2, z: 4, core: 2. Of those that a mesh axis runs over, the one named last changes fastest.
Arguments:
- tokens: bfloat16 [8, 2048, 1536], P('shard', 'ctx'), may hold values from -6 to 6
- segments: int32 [8, 2048], P('shard'), may hold values from 0 to 127, as said below
- assign: int32 [16], replicated, may hold values from 0 to 15, each once
- w_qkv: bfloat16 [1536, 1792], P('shard'), may hold values from -0.15625 to 0.15625
- w_out: bfloat16 [1536, 1536], P('shard'), may hold values from -1.25 to 1.25
- w_gate_up: bfloat16 [1536, 9216], P('shard'), may hold values from -0.15625 to 0.15625
- w_down: bfloat16 [4608, 1536], P('shard'), may hold values from -0.09375 to 0.09375
- gain_attn: bfloat16 [1536], P('shard'), may hold values from 0.099609375 to 1.8984375
- gain_ffn: bfloat16 [1536], P('shard'), may hold values from 0.099609375 to 1.8984375
- cotangent: bfloat16 [8, 2048, 1536], P('shard', 'ctx'), may hold values from -6 to 6
Outputs:
- output: float32 [8, 2048, 1536], P('shard', 'ctx')
- input_grad: float32 [8, 2048, 1536], P('shard', 'ctx')
- grad_qkv: float32 [1536, 1792], P('shard')
- grad_out: float32 [1536, 1536], P('shard')
- grad_gate_up: float32 [1536, 9216], P('shard')
- grad_down: float32 [4608, 1536], P('shard')
- grad_gain_attn: float32 [1536], P('shard')
- grad_gain_ffn: float32 [1536], P('shard')
The draws below stay inside these ranges and needn't reach their ends.
Inputs may be any that keep to these rules, and one draw needn't show every extreme that they name: `segments`: within each sequence the numbers start at 0 and never fall; of the 2 sequences at one index of shard, at least one is a single document; some sequence reaches the largest number.
All inputs are finite; a program needn't handle non-finite values.
Results may differ from the reference program's by a relative error of at most 0.018.
Values may be sent and summed in bfloat16 or wider, within the bound.
No kernel may reach another device: no remote copies, remote signals or barrier semaphores. Data moves between devices by JAX's collectives and lax.ppermute only.
A program may use at most 256 MiB of HBM per device.

```python
import math
import jax
import jax.numpy as jnp
from jax import lax

D = 1536
H = 12
HD = 128
FF = 4608
W = 1024
BLK = 128
SEQ_G = 2
BLOCKS = 16
LEN = 2048
SEQS = 8
N_SHARD = 4


def draw_segments(key, part):
    total_seqs = SEQ_G * N_SHARD
    rate_key = jax.random.fold_in(key, 11)
    flag_key = jax.random.fold_in(key, 12)
    pick_key = jax.random.fold_in(key, 13)
    spacing = 2 ** jax.random.randint(rate_key, (total_seqs, 1), 4, 11)
    raw_bits = jax.random.randint(flag_key, (total_seqs, LEN), 0, 1048576)
    flags = (raw_bits % spacing == 0).astype(jnp.int32)
    whole_pick = jax.random.randint(pick_key, (N_SHARD, 1), 0, SEQ_G)
    chosen = (jnp.arange(SEQ_G, dtype=jnp.int32)[None, :] == whole_pick).reshape(total_seqs, 1)
    dense_index = (whole_pick[0, 0] + 1) % SEQ_G
    dense_row = (jnp.arange(total_seqs, dtype=jnp.int32) == dense_index)[:, None]
    positions = jnp.arange(LEN, dtype=jnp.int32)[None, :]
    dense_flags = (positions % 16 == 0).astype(jnp.int32)
    flags = jnp.where(dense_row, dense_flags, flags)
    flags = jnp.where(chosen, 0, flags)
    flags = flags.at[:, 0].set(0)
    return jnp.minimum(jnp.cumsum(flags, axis=1), LEN // 16 - 1).astype(jnp.int32)


def shard_levels(rng, dims, pieces, low, largest):
    level, own = 1.0, jax.random.fold_in(rng, 6)
    for axis_at, parts in pieces:
        steps = jnp.exp(jax.random.uniform(jax.random.fold_in(own, axis_at), (parts,), jnp.float32, low / len(pieces), largest / len(pieces)))
        level = level * jnp.repeat(steps, dims[axis_at] // parts).reshape([-1 if axis == axis_at else 1 for axis in range(len(dims))])
    return level


def centred(key, extent, spread, reach, cuts=(), held_as=jnp.bfloat16):
    gain = shard_levels(key, extent, cuts, -0.22, 0.18) if cuts else 1.0
    values = jax.random.normal(key, extent, jnp.float32) * spread * gain
    return jnp.minimum(jnp.maximum(values, -reach), reach).astype(held_as)


def setup_inputs(seed: int = 0) -> dict:
    key_of = jax.random.split(jax.random.key(seed), 11)
    return {
        "tokens": centred(key_of[0], (SEQS, LEN, D), 1.0, 6.0, ((0, 4), (1, 8))),
        "segments": draw_segments(jax.random.fold_in(key_of[10], 71), 0),
        "assign": jax.random.permutation(key_of[2], BLOCKS).astype(jnp.int32),
        "w_qkv": centred(key_of[3], (D, H * HD + 2 * HD), D ** -0.5, 0.15625, ((0, 4),)),
        "w_out": centred(key_of[4], (H * HD, D), (H * HD // 64) ** -0.5, 1.25, ((0, 4),)),
        "w_gate_up": centred(key_of[5], (D, 2 * FF), D ** -0.5, 0.15625, ((0, 4),)),
        "w_down": centred(key_of[6], (FF, D), FF ** -0.5, 0.09375, ((0, 4),)),
        "gain_attn": jnp.clip(1.0 + 0.18 * jax.random.normal(key_of[7], (D,), jnp.float32), 0.099609375, 1.8984375).astype(jnp.bfloat16),
        "gain_ffn": jnp.clip(1.0 + 0.18 * jax.random.normal(key_of[8], (D,), jnp.float32), 0.099609375, 1.8984375).astype(jnp.bfloat16),
        "cotangent": centred(key_of[9], (SEQS, LEN, D), 1.0, 6.0, ((0, 4), (1, 8))),
    }


@jax.custom_vjp
def low(v):
    return lax.optimization_barrier(v.astype(jnp.bfloat16)).astype(jnp.float32)

@jax.custom_vjp
def low_back(v):
    return v

def low_keep(v):
    return (low(v), None)

def low_pass(kept, grad):
    return (grad,)

def back_keep(v):
    return (v, None)

def back_low(kept, grad):
    return (low(grad),)
low.defvjp(low_keep, low_pass)
low_back.defvjp(back_keep, back_low)
epsilon = 1e-06
masked_score = -1e+30
highest = lax.Precision.HIGHEST

def norm_hat(tok_rows):
    return tok_rows * lax.rsqrt(lax.optimization_barrier(jnp.mean(tok_rows * tok_rows, axis=-1, keepdims=True)) + epsilon)

def attend_block(queries, key_rows, value_rows, seq_segs, block_id):
    block_rows = queries.shape[0]
    length = key_rows.shape[0]
    offset = block_id * block_rows
    query_pos = offset + jnp.arange(block_rows, dtype=jnp.int32)
    key_pos = jnp.arange(length, dtype=jnp.int32)
    query_seg = lax.dynamic_slice_in_dim(seq_segs, offset, block_rows, 0)
    raw = jnp.einsum('qhd,kd->hqk', queries, key_rows, precision=highest)
    scores = low_back(raw) * HD ** (-0.5)
    allowed = (query_seg[:, None] == seq_segs[None, :]) & (key_pos[None, :] <= query_pos[:, None]) & (query_pos[:, None] - key_pos[None, :] < W)
    scores = jnp.where(allowed[None], scores, masked_score)
    row_max = lax.optimization_barrier(jnp.max(scores, axis=-1, keepdims=True))
    expo_vals = jnp.exp(scores - row_max)
    attn_probs = expo_vals / lax.optimization_barrier(jnp.sum(expo_vals, axis=-1, keepdims=True))
    return jnp.einsum('hqk,kd->qhd', low(attn_probs), value_rows, precision=highest)

def layer_seq(seq_rows, seq_segs, qkv_f, out_f, gate_up_f, down_f, attn_gain, ffn_gain):
    length = seq_rows.shape[0]
    normed = low(norm_hat(seq_rows) * attn_gain)
    qkv_rows = low_back(low(jnp.dot(normed, qkv_f, precision=highest)))
    queries = qkv_rows[:, :H * HD].reshape(length, H, HD)
    key_rows = qkv_rows[:, H * HD:H * HD + HD]
    value_rows = qkv_rows[:, H * HD + HD:]
    block_rows = math.gcd(512, length)
    checked = jax.checkpoint(attend_block)

    def one_block(block_id):
        query_block = lax.dynamic_slice_in_dim(queries, block_id * block_rows, block_rows, 0)
        return checked(query_block, key_rows, value_rows, seq_segs, block_id)
    mixed = lax.map(one_block, jnp.arange(length // block_rows, dtype=jnp.int32))
    mixed = low_back(low(mixed.reshape(length, H * HD)))
    hidden = seq_rows + low_back(jnp.dot(mixed, out_f, precision=highest))
    normed_two = low(norm_hat(hidden) * ffn_gain)
    gate_up = low_back(jnp.dot(normed_two, gate_up_f, precision=highest))
    active = low(jax.nn.gelu(gate_up[:, :FF], approximate=True) * gate_up[:, FF:])
    return hidden + low_back(jnp.dot(active, down_f, precision=highest))

def reference(tokens, segments, assign, w_qkv, w_out, w_gate_up, w_down, gain_attn, gain_ffn, cotangent):
    seq_count = tokens.shape[0]

    def to_natural(stored):
        block_view = stored.reshape(seq_count, BLOCKS, BLK, stored.shape[-1])
        return jnp.zeros_like(block_view).at[:, assign].set(block_view).reshape(stored.shape)

    def to_stored(natural):
        return natural.reshape(seq_count, BLOCKS, BLK, natural.shape[-1])[:, assign].reshape(natural.shape)
    inputs = to_natural(tokens.astype(jnp.float32))
    outgrad = to_natural(cotangent.astype(jnp.float32))

    def forward(rows_all, qkv_f, out_f, gate_up_f, down_f, attn_gain, ffn_gain):

        def per_seq(seq_item):
            return layer_seq(seq_item[0], seq_item[1], qkv_f, out_f, gate_up_f, down_f, attn_gain, ffn_gain)
        return lax.map(per_seq, (rows_all, segments))
    result, pull_back = jax.vjp(forward, inputs, w_qkv.astype(jnp.float32), w_out.astype(jnp.float32), w_gate_up.astype(jnp.float32), w_down.astype(jnp.float32), gain_attn.astype(jnp.float32), gain_ffn.astype(jnp.float32))
    grads = pull_back(outgrad)
    return (to_stored(result), to_stored(grads[0]), grads[1], grads[2], grads[3], grads[4], grads[5], grads[6])
```

```python
import functools

import jax
import jax.numpy as jnp
from jax import lax
from jax.experimental import pallas as pl
from jax.experimental.pallas import tpu as pltpu
from jax.sharding import PartitionSpec as P

H = 12
HD = 128
FF = 4608
W = 1024
BLK = 128
BACK = W // BLK
QW = H * HD

epsilon = 1e-06
masked_score = -1e30
scale = HD ** (-0.5)
log2e = 1.4426950408889634


def dot_f32(left, right, dims=((1,), (0,))):
    return lax.dot_general(left, right, (dims, ((), ())), preferred_element_type=jnp.float32)


def inv_rms(rows):
    return lax.rsqrt(jnp.mean(rows * rows, axis=-1, keepdims=True) + epsilon)


def add_low(a, b):
    return (a.astype(jnp.float32) + b.astype(jnp.float32)).astype(jnp.bfloat16)


def stack_heads(dst, src):
    for h in range(H):
        dst[h * BLK : (h + 1) * BLK, :] = src[0, :, h * HD : (h + 1) * HD]


def block_bias(seg_ref, seq, q_block, k_block, step):
    q_seg = jnp.broadcast_to(seg_ref[seq, q_block], (BLK, BLK))
    k_seg = jnp.broadcast_to(seg_ref[seq, k_block], (BLK, BLK)).T
    allowed = q_seg == k_seg
    if step in (0, BACK):
        key_at = lax.broadcasted_iota(jnp.int32, (BLK, BLK), 0)
        query_at = lax.broadcasted_iota(jnp.int32, (BLK, BLK), 1)
        allowed &= key_at <= query_at if step == BACK else key_at > query_at
    bias = jnp.where(allowed, 0.0, masked_score)
    return jnp.concatenate([bias] * H, axis=1)


def fold8(v, how):
    return how(v.reshape(BLK // 8, 8, QW), axis=0)


def attend_kernel(
    blk_ref, low_ref, slot_ref, half_ref, q_ref, kv_ref, seg_ref, o_ref, lse_ref, qs, sc, mx, tot, acc
):
    seq, mine = pl.program_id(0), pl.program_id(1)
    q_block = blk_ref[mine]
    lowest = low_ref[seq * 2 + mine]
    stack_heads(qs, q_ref)
    mx[...] = jnp.full(mx.shape, masked_score, jnp.float32)
    tot[...] = jnp.zeros_like(tot)
    acc[...] = jnp.zeros_like(acc)
    for step in range(BACK + 1):
        k_block = q_block - BACK + step

        @pl.when(k_block >= lowest)
        def _(step=step, k_block=k_block):
            keys = kv_ref[slot_ref[k_block], seq, half_ref[k_block], :, :HD]
            s = dot_f32(keys, qs[...], ((1,), (1,))) * (scale * log2e)
            s += block_bias(seg_ref, seq, q_block, k_block, step)
            sc[step * BLK : (step + 1) * BLK, :] = s
            mx[...] = jnp.maximum(mx[...], fold8(s, jnp.max))

    top = jnp.max(mx[...], axis=0, keepdims=True)
    for step in range(BACK + 1):
        k_block = q_block - BACK + step

        @pl.when(k_block >= lowest)
        def _(step=step, k_block=k_block):
            vals = kv_ref[slot_ref[k_block], seq, half_ref[k_block], :, HD:]
            p = jnp.exp2(sc[step * BLK : (step + 1) * BLK, :] - top)
            tot[...] += fold8(p, jnp.sum)
            acc[...] += dot_f32(vals, p.astype(jnp.bfloat16), ((0,), (0,)))

    total = jnp.sum(tot[...], axis=0, keepdims=True)
    out = acc[...] / total
    for h in range(H):
        o_ref[0, :, h * HD : (h + 1) * HD] = out[:, h * BLK : (h + 1) * BLK].T.astype(jnp.bfloat16)
    lse_ref[0, 0] = top + jnp.log2(total)


def attend_back_kernel(
    blk_ref, low_ref, slot_ref, half_ref, q_ref, do_ref, o_ref, kv_ref, seg_ref, lse_ref,
    dq_ref, dkv_ref, qs, dos, dqt, dacc,
):
    seq, mine = pl.program_id(0), pl.program_id(1)
    q_block = blk_ref[mine]
    lowest = low_ref[seq * 2 + mine]

    @pl.when((seq == 0) & (mine == 0))
    def _():
        dacc[...] = jnp.zeros_like(dacc)

    stack_heads(qs, q_ref)
    stack_heads(dos, do_ref)
    dqt[...] = jnp.zeros_like(dqt)
    deltas = []
    for h in range(H):
        cols = slice(h * HD, (h + 1) * HD)
        both = do_ref[0, :, cols].astype(jnp.float32) * o_ref[0, :, cols].astype(jnp.float32)
        deltas.append(jnp.sum(both.T, axis=0, keepdims=True))
    delta = jnp.concatenate(deltas, axis=1)
    lse = lse_ref[0, 0]
    for step in range(BACK + 1):
        k_block = q_block - BACK + step

        @pl.when(k_block >= lowest)
        def _(step=step, k_block=k_block):
            slot, half = slot_ref[k_block], half_ref[k_block]
            keys = kv_ref[slot, seq, half, :, :HD]
            vals = kv_ref[slot, seq, half, :, HD:]
            s = dot_f32(keys, qs[...], ((1,), (1,))) * (scale * log2e)
            p = jnp.exp2(s + block_bias(seg_ref, seq, q_block, k_block, step) - lse)
            dp = dot_f32(vals, dos[...], ((1,), (1,)))
            d_raw = (p * (dp - delta)).astype(jnp.bfloat16)
            dqt[...] += dot_f32(keys, d_raw, ((0,), (0,)))
            dacc[slot, seq, half, :, :HD] += dot_f32(d_raw, qs[...]) * scale
            dacc[slot, seq, half, :, HD:] += dot_f32(p.astype(jnp.bfloat16), dos[...])

    out = dqt[...] * scale
    for h in range(H):
        dq_ref[0, :, h * HD : (h + 1) * HD] = out[:, h * BLK : (h + 1) * BLK].T.astype(jnp.bfloat16)

    @pl.when((seq == pl.num_programs(0) - 1) & (mine == 1))
    def _():
        dkv_ref[...] = dacc[...].astype(jnp.bfloat16)


def whole_spec(shape):
    return pl.BlockSpec(shape, lambda s, m, *_: (0,) * len(shape))


def row_spec():
    return pl.BlockSpec((1, BLK, QW), lambda s, m, *_: (s, m, 0))


lse_spec = pl.BlockSpec((1, 1, 1, QW), lambda s, m, *_: (s, m, 0, 0))
kernel_params = pltpu.CompilerParams(vmem_limit_bytes=48 * 2**20)


def attend(scalars, qkv, key_value, seg):
    seqs, rows = qkv.shape[:2]
    return pl.pallas_call(
        attend_kernel,
        grid_spec=pltpu.PrefetchScalarGridSpec(
            num_scalar_prefetch=4,
            grid=(seqs, 2),
            in_specs=[row_spec(), whole_spec(key_value.shape), whole_spec(seg.shape)],
            out_specs=[row_spec(), lse_spec],
            scratch_shapes=[
                pltpu.VMEM((QW, HD), jnp.bfloat16),
                pltpu.VMEM((W + BLK, QW), jnp.float32),
                pltpu.VMEM((8, QW), jnp.float32),
                pltpu.VMEM((8, QW), jnp.float32),
                pltpu.VMEM((HD, QW), jnp.float32),
            ],
        ),
        out_shape=[
            jax.ShapeDtypeStruct((seqs, rows, QW), jnp.bfloat16),
            jax.ShapeDtypeStruct((seqs, 2, 1, QW), jnp.float32),
        ],
        compiler_params=kernel_params,
        cost_estimate=pl.CostEstimate(flops=7 * 10**9, bytes_accessed=8 * 2**20, transcendentals=7 * 10**6),
        name="attend",
    )(*scalars, qkv, key_value, seg)


def attend_back(scalars, qkv, d_mixed, mixed, key_value, seg, lse):
    seqs, rows = qkv.shape[:2]
    return pl.pallas_call(
        attend_back_kernel,
        grid_spec=pltpu.PrefetchScalarGridSpec(
            num_scalar_prefetch=4,
            grid=(seqs, 2),
            in_specs=[row_spec(), row_spec(), row_spec(), whole_spec(key_value.shape), whole_spec(seg.shape), lse_spec],
            out_specs=[row_spec(), whole_spec(key_value.shape)],
            scratch_shapes=[
                pltpu.VMEM((QW, HD), jnp.bfloat16),
                pltpu.VMEM((QW, HD), jnp.bfloat16),
                pltpu.VMEM((HD, QW), jnp.float32),
                pltpu.VMEM(key_value.shape, jnp.float32),
            ],
        ),
        out_shape=[
            jax.ShapeDtypeStruct((seqs, rows, QW), jnp.bfloat16),
            jax.ShapeDtypeStruct(key_value.shape, jnp.bfloat16),
        ],
        compiler_params=kernel_params,
        cost_estimate=pl.CostEstimate(flops=18 * 10**9, bytes_accessed=12 * 2**20, transcendentals=7 * 10**6),
        name="attend_back",
    )(*scalars, qkv, d_mixed, mixed, key_value, seg, lse)


class Plan:
    def __init__(self, mesh):
        self.shards = mesh.shape["shard"]
        self.ctxs = mesh.shape["ctx"]
        half = self.ctxs // 2
        self.ring = [2 * z for z in range(half)] + [2 * z + 1 for z in reversed(range(half))]
        self.place = [self.ring.index(c) for c in range(self.ctxs)]
        self.right = [(self.ring[i], self.ring[(i + 1) % self.ctxs]) for i in range(self.ctxs)]
        self.left = [(b, a) for a, b in self.right]
        self.bits = [1 << b for b in range(self.shards.bit_length() - 1)]

    def my_place(self):
        table = jnp.array(self.place, jnp.int32)
        at = jnp.arange(self.ctxs, dtype=jnp.int32) == lax.axis_index("ctx")
        return jnp.sum(jnp.where(at, table, 0))

    def swap(self, v, bit):
        return lax.ppermute(v, "shard", [(i, i ^ bit) for i in range(self.shards)])

    def my_bit(self, bit):
        return (lax.axis_index("shard") // bit) % 2

    def gather_xor(self, v):
        pieces = {0: v}
        for bit in reversed(self.bits):
            pieces |= {j | bit: self.swap(p, bit) for j, p in pieces.items()}
        return [pieces[j] for j in range(self.shards)]

    def scatter_xor(self, pieces):
        pieces = dict(enumerate(pieces))
        for bit in self.bits:
            got = {j ^ bit: self.swap(pieces[j], bit) for j in sorted(pieces, reverse=True) if j & bit}
            pieces = {j: add_low(pieces[j], got[j]) for j in got}
        return pieces[0]

    def gather_rows(self, v):
        out = v[None]
        for bit in reversed(self.bits):
            other = self.swap(out, bit)
            first = self.my_bit(bit) == 0
            out = jnp.stack([jnp.where(first, out, other), jnp.where(first, other, out)], axis=1)
            out = out.reshape(-1, *v.shape)
        return out.reshape(-1, *v.shape[1:])

    def scatter_rows(self, v, add=add_low):
        cur = v.reshape(self.shards, v.shape[0] // self.shards, *v.shape[1:])
        for bit in self.bits:
            pairs = cur.reshape(cur.shape[0] // 2, 2, *cur.shape[1:])
            mine = self.my_bit(bit)
            keep = lax.dynamic_index_in_dim(pairs, mine, 1, False)
            give = lax.dynamic_index_in_dim(pairs, 1 - mine, 1, False)
            cur = add(keep, self.swap(give, bit))
        return cur[0]

    def exchange_columns(self, v, blocks):
        me = lax.axis_index("shard")
        own = blocks(me)
        out = jnp.zeros((self.shards, *own.shape), own.dtype)
        out = lax.dynamic_update_index_in_dim(out, own, me, 0)
        for j in range(1, self.shards):
            other = me ^ j
            out = lax.dynamic_update_index_in_dim(out, self.swap(blocks(other), j), other, 0)
        return out

    def ring_gather(self, v):
        n = self.ctxs
        pieces = {0: v}
        a = b = v
        for step in range(1, n // 2 + 1):
            a = lax.ppermute(a, "ctx", self.right)
            pieces[step] = a
            if n - step > n // 2:
                b = lax.ppermute(b, "ctx", self.left)
                pieces[n - step] = b
        return jnp.stack([pieces[k] for k in range(n)])

    def ring_scatter(self, v):
        n = self.ctxs
        a, b = v[n // 2], v[n // 2 - 1]
        for step in range(n // 2 + 1, n + 1):
            a = lax.ppermute(a, "ctx", self.right)
            a = add_low(a, v[step % n])
        for step in range(n // 2 - 2, -1, -1):
            b = lax.ppermute(b, "ctx", self.left)
            if step:
                b = add_low(b, v[step])
        return a.astype(jnp.float32) + b.astype(jnp.float32)

    def ring_sum(self, v):
        n = self.ctxs
        rows, cols = v.shape
        cut = cols // 2
        place = self.my_place()
        chunks = v.reshape(n, rows // n, cols)

        def part(k, way):
            at = chunks[:, :, :cut] if way > 0 else chunks[:, :, cut:]
            return lax.dynamic_index_in_dim(at, lax.rem(place - way * k + 2 * n, n), 0, False)

        a, b = part(1, 1), part(1, -1)
        for step in range(2, n + 1):
            a = add_low(lax.ppermute(a, "ctx", self.right), part(step, 1))
            b = add_low(lax.ppermute(b, "ctx", self.left), part(step, -1))
        out = jnp.zeros(chunks.shape, jnp.float32)

        def put(out, piece, k, way):
            at = lax.rem(place - way * k + 2 * n, n)
            return lax.dynamic_update_slice(
                out, piece.astype(jnp.float32)[None], (at, 0, 0 if way > 0 else cut)
            )

        out = put(put(out, a, 0, 1), b, 0, -1)
        for step in range(1, n):
            a = lax.ppermute(a, "ctx", self.right)
            b = lax.ppermute(b, "ctx", self.left)
            out = put(put(out, a, step, 1), b, step, -1)
        return out.reshape(rows, cols)

    def small_sum(self, v):
        mine = self.scatter_rows(v, lambda a, b: a + b)
        bit = 1
        while bit < self.ctxs:
            mine = mine + lax.ppermute(mine, "ctx", [(c, c ^ bit) for c in range(self.ctxs)])
            bit *= 2
        return mine


def body(plan, tokens, segments, assign, w_qkv, w_out, w_gate_up, w_down, gain_attn, gain_ffn, cotangent):
    seqs, rows_dev, width = tokens.shape
    rows = seqs * rows_dev
    blocks = assign.shape[0]
    n = plan.shards
    ffn = FF // n
    low = jnp.bfloat16
    ids = jnp.arange(blocks, dtype=jnp.int32)
    my_blocks = lax.dynamic_slice_in_dim(assign, 2 * lax.axis_index("ctx"), 2, 0)
    place_of = jnp.array([plan.place[i // 2] for i in range(blocks)], jnp.int32)
    back = lax.rem(plan.my_place() - place_of + plan.ctxs, plan.ctxs)
    hit = assign[None, :] == ids[:, None]
    slot_of = jnp.sum(jnp.where(hit, back[None, :], 0), axis=1)
    half_of = jnp.sum(jnp.where(hit, (ids % 2)[None, :], 0), axis=1)
    firsts = jnp.stack([lax.dynamic_index_in_dim(segments, my_blocks[m] * BLK, 1, False) for m in range(2)], 1)
    starts = jnp.sum((segments[:, None, :] < firsts[:, :, None]).astype(jnp.int32), axis=2)
    lowest = jnp.maximum(jnp.maximum(starts // BLK, my_blocks[None, :] - BACK), 0).reshape(-1)
    scalars = (my_blocks, lowest, slot_of, half_of)
    seg = segments.astype(jnp.float32).reshape(seqs, blocks, 1, BLK)

    gains = plan.gather_rows(jnp.stack([gain_attn, gain_ffn], 1)).astype(jnp.float32)
    gain_one, gain_two = gains[:, 0], gains[:, 1]
    w_kv = plan.gather_rows(w_qkv[:, QW:])
    w_q = plan.gather_rows(w_qkv[:, :QW])
    w_o = plan.gather_rows(w_out)

    def gu_block(t):
        g = lax.dynamic_slice_in_dim(w_gate_up, t * ffn, ffn, 1)
        u = lax.dynamic_slice_in_dim(w_gate_up, FF + t * ffn, ffn, 1)
        return jnp.concatenate([g, u], axis=1)

    w_gu = plan.exchange_columns(w_gate_up, gu_block).reshape(width, 2 * ffn)

    tok = tokens.reshape(rows, width).astype(jnp.float32)
    scale_one = inv_rms(tok)
    hat_one = tok * scale_one
    normed_one = (hat_one * gain_one).astype(low)
    key_value = dot_f32(normed_one, w_kv).astype(low).reshape(seqs, 2, BLK, 2 * HD)
    kv_all = plan.ring_gather(key_value)
    queries = dot_f32(normed_one, w_q).astype(low).reshape(seqs, rows_dev, QW)
    mixed, lse = attend(scalars, queries, kv_all, seg)
    mixed_low = mixed.reshape(rows, QW)
    hidden = tok + dot_f32(mixed_low, w_o)
    scale_two = inv_rms(hidden)
    hat_two = hidden * scale_two
    normed_two = (hat_two * gain_two).astype(low)

    grad_low = cotangent.reshape(rows, width)
    n2 = jnp.concatenate(plan.gather_xor(normed_two))
    gy = jnp.concatenate(plan.gather_xor(grad_low))
    gate_up = dot_f32(n2, w_gu)
    d_act = dot_f32(gy, w_down, ((1,), (1,)))

    def gelu_product(gate_in, up_in):
        return jax.nn.gelu(gate_in, approximate=True) * up_in

    act, pull = jax.vjp(gelu_product, gate_up[:, :ffn], gate_up[:, ffn:])
    act = act.astype(low)
    d_gu = jnp.concatenate(pull(d_act), axis=1).astype(low)
    grad_down = plan.ring_sum(dot_f32(act, gy, ((0,), (0,))).astype(low))
    d_n2 = dot_f32(d_gu, w_gu, ((1,), (1,))).astype(low)
    d_normed_two = plan.scatter_xor([d_n2[j * rows : (j + 1) * rows] for j in range(n)]).astype(jnp.float32)
    part_gu = dot_f32(n2, d_gu, ((0,), (0,))).astype(low)
    me = lax.axis_index("shard")
    own_gu = plan.exchange_columns(
        part_gu, lambda t: lax.dynamic_slice_in_dim(part_gu, t * (width // n), width // n, 0)
    )
    summed = plan.ring_sum(own_gu.reshape(n * (width // n), 2 * ffn))
    summed = summed.reshape(n, width // n, 2, ffn)
    grad_gate_up = jnp.moveaxis(summed, 0, 2).reshape(width // n, 2 * FF)
    down = dot_f32(act, w_down).astype(low)
    branch = plan.scatter_xor([down[j * rows : (j + 1) * rows] for j in range(n)]).astype(jnp.float32)
    output = (hidden + branch).reshape(seqs, rows_dev, width)

    grad_gain_ffn = plan.small_sum(jnp.sum(d_normed_two * hat_two, axis=0))
    e = d_normed_two * gain_two
    d_hidden = grad_low.astype(jnp.float32) + scale_two * (
        e - hat_two * jnp.mean(e * hat_two, axis=-1, keepdims=True)
    )
    d_branch = d_hidden.astype(low)
    d_mixed = dot_f32(d_branch, w_o, ((1,), (1,))).astype(low).reshape(seqs, rows_dev, QW)
    dq, dkv = attend_back(scalars, queries, d_mixed, mixed, kv_all, seg, lse)
    dkv_own = plan.ring_scatter(dkv)
    d_qkv = jnp.concatenate([dq.reshape(rows, QW), dkv_own.astype(low).reshape(rows, 2 * HD)], axis=1)
    part_out = plan.scatter_rows(dot_f32(mixed_low, d_branch, ((0,), (0,))).astype(low))
    grad_out = plan.ring_sum(part_out)
    part_qkv = plan.scatter_rows(dot_f32(normed_one, d_qkv, ((0,), (0,))).astype(low))
    grad_qkv = plan.ring_sum(part_qkv)
    d_normed_one = dot_f32(dq.reshape(rows, QW), w_q, ((1,), (1,))) + dot_f32(
        d_qkv[:, QW:], w_kv, ((1,), (1,))
    )
    grad_gain_attn = plan.small_sum(jnp.sum(d_normed_one * hat_one, axis=0))
    f = d_normed_one * gain_one
    input_grad = d_hidden + scale_one * (f - hat_one * jnp.mean(f * hat_one, axis=-1, keepdims=True))
    return (
        output,
        input_grad.reshape(seqs, rows_dev, width),
        grad_qkv,
        grad_out,
        grad_gate_up,
        grad_down,
        grad_gain_attn,
        grad_gain_ffn,
    )


def solution(mesh):
    return jax.shard_map(
        functools.partial(body, Plan(mesh)),
        mesh=mesh,
        in_specs=(
            P("shard", "ctx", None),
            P("shard", None),
            P(),
            P("shard", None),
            P("shard", None),
            P("shard", None),
            P("shard", None),
            P("shard"),
            P("shard"),
            P("shard", "ctx", None),
        ),
        out_specs=(
            P("shard", "ctx", None),
            P("shard", "ctx", None),
            P("shard", None),
            P("shard", None),
            P("shard", None),
            P("shard", None),
            P("shard"),
            P("shard"),
        ),
        check_vma=False,
    )
```

```python
import functools

import jax
import jax.numpy as jnp
from jax import lax
from jax.experimental import pallas as pl
from jax.experimental.pallas import tpu as pltpu
from jax.sharding import PartitionSpec as P

H = 12
HD = 128
FF = 4608
W = 1024
BLK = 128
BACK = W // BLK
QW = H * HD

epsilon = 1e-06
masked_score = -1e30
scale = HD ** (-0.5)
log2e = 1.4426950408889634
gelu_c = 0.7978845608028654
gelu_a = 0.044715


def dot_f32(left, right, dims=((1,), (0,))):
    return lax.dot_general(left, right, (dims, ((), ())), preferred_element_type=jnp.float32)


def inv_rms(rows):
    return lax.rsqrt(jnp.mean(rows * rows, axis=-1, keepdims=True) + epsilon)


def add_low(a, b):
    return (a.astype(jnp.float32) + b.astype(jnp.float32)).astype(jnp.bfloat16)


def stack_heads(dst, src):
    for h in range(H):
        dst[h * BLK : (h + 1) * BLK, :] = src[0, :, h * HD : (h + 1) * HD]


def block_bias(seg_ref, seq, q_block, k_block, step):
    q_seg = jnp.broadcast_to(seg_ref[seq, q_block], (BLK, BLK))
    k_seg = jnp.broadcast_to(seg_ref[seq, k_block], (BLK, BLK)).T
    allowed = q_seg == k_seg
    if step in (0, BACK):
        key_at = lax.broadcasted_iota(jnp.int32, (BLK, BLK), 0)
        query_at = lax.broadcasted_iota(jnp.int32, (BLK, BLK), 1)
        allowed &= key_at <= query_at if step == BACK else key_at > query_at
    bias = jnp.where(allowed, 0.0, masked_score)
    return jnp.concatenate([bias] * H, axis=1)


def fold8(v, how):
    return how(v.reshape(BLK // 8, 8, QW), axis=0)


def attend_kernel(
    blk_ref, low_ref, slot_ref, half_ref, q_ref, kv_ref, seg_ref, o_ref, lse_ref, qs, sc, mx, tot, acc
):
    seq, mine = pl.program_id(0), pl.program_id(1)
    q_block = blk_ref[mine]
    lowest = low_ref[seq * 2 + mine]
    stack_heads(qs, q_ref)
    mx[...] = jnp.full(mx.shape, masked_score, jnp.float32)
    tot[...] = jnp.zeros_like(tot)
    acc[...] = jnp.zeros_like(acc)
    for step in range(BACK + 1):
        k_block = q_block - BACK + step

        @pl.when(k_block >= lowest)
        def _(step=step, k_block=k_block):
            keys = kv_ref[slot_ref[k_block], seq, half_ref[k_block], :, :HD]
            s = dot_f32(keys, qs[...], ((1,), (1,))) * (scale * log2e)
            s += block_bias(seg_ref, seq, q_block, k_block, step)
            sc[step * BLK : (step + 1) * BLK, :] = s
            mx[...] = jnp.maximum(mx[...], fold8(s, jnp.max))

    top = jnp.max(mx[...], axis=0, keepdims=True)
    for step in range(BACK + 1):
        k_block = q_block - BACK + step

        @pl.when(k_block >= lowest)
        def _(step=step, k_block=k_block):
            vals = kv_ref[slot_ref[k_block], seq, half_ref[k_block], :, HD:]
            p = jnp.exp2(sc[step * BLK : (step + 1) * BLK, :] - top)
            tot[...] += fold8(p, jnp.sum)
            acc[...] += dot_f32(vals, p.astype(jnp.bfloat16), ((0,), (0,)))

    total = jnp.sum(tot[...], axis=0, keepdims=True)
    out = acc[...] / total
    for h in range(H):
        o_ref[0, :, h * HD : (h + 1) * HD] = out[:, h * BLK : (h + 1) * BLK].T.astype(jnp.bfloat16)
    lse_ref[0, 0] = top + jnp.log2(total)


def attend_back_kernel(
    blk_ref, low_ref, slot_ref, half_ref, q_ref, do_ref, o_ref, kv_ref, seg_ref, lse_ref,
    dq_ref, dkv_ref, qs, dos, dqt, dacc,
):
    seq, mine = pl.program_id(0), pl.program_id(1)
    q_block = blk_ref[mine]
    lowest = low_ref[seq * 2 + mine]

    @pl.when((seq == 0) & (mine == 0))
    def _():
        dacc[...] = jnp.zeros_like(dacc)

    stack_heads(qs, q_ref)
    stack_heads(dos, do_ref)
    dqt[...] = jnp.zeros_like(dqt)
    deltas = []
    for h in range(H):
        cols = slice(h * HD, (h + 1) * HD)
        both = do_ref[0, :, cols].astype(jnp.float32) * o_ref[0, :, cols].astype(jnp.float32)
        deltas.append(jnp.sum(both.T, axis=0, keepdims=True))
    delta = jnp.concatenate(deltas, axis=1)
    lse = lse_ref[0, 0]
    for step in range(BACK + 1):
        k_block = q_block - BACK + step

        @pl.when(k_block >= lowest)
        def _(step=step, k_block=k_block):
            slot, half = slot_ref[k_block], half_ref[k_block]
            keys = kv_ref[slot, seq, half, :, :HD]
            vals = kv_ref[slot, seq, half, :, HD:]
            s = dot_f32(keys, qs[...], ((1,), (1,))) * (scale * log2e)
            p = jnp.exp2(s + block_bias(seg_ref, seq, q_block, k_block, step) - lse)
            dp = dot_f32(vals, dos[...], ((1,), (1,)))
            d_raw = (p * (dp - delta)).astype(jnp.bfloat16)
            dqt[...] += dot_f32(keys, d_raw, ((0,), (0,)))
            dacc[slot, seq, half, :, :HD] += dot_f32(d_raw, qs[...]) * scale
            dacc[slot, seq, half, :, HD:] += dot_f32(p.astype(jnp.bfloat16), dos[...])

    out = dqt[...] * scale
    for h in range(H):
        dq_ref[0, :, h * HD : (h + 1) * HD] = out[:, h * BLK : (h + 1) * BLK].T.astype(jnp.bfloat16)

    @pl.when((seq == pl.num_programs(0) - 1) & (mine == 1))
    def _():
        dkv_ref[...] = dacc[...].astype(jnp.bfloat16)


def whole_spec(shape):
    return pl.BlockSpec(shape, lambda s, m, *_: (0,) * len(shape))


def row_spec():
    return pl.BlockSpec((1, BLK, QW), lambda s, m, *_: (s, m, 0))


lse_spec = pl.BlockSpec((1, 1, 1, QW), lambda s, m, *_: (s, m, 0, 0))
kernel_params = pltpu.CompilerParams(vmem_limit_bytes=48 * 2**20)


def attend(scalars, qkv, key_value, seg):
    seqs, rows = qkv.shape[:2]
    return pl.pallas_call(
        attend_kernel,
        grid_spec=pltpu.PrefetchScalarGridSpec(
            num_scalar_prefetch=4,
            grid=(seqs, 2),
            in_specs=[row_spec(), whole_spec(key_value.shape), whole_spec(seg.shape)],
            out_specs=[row_spec(), lse_spec],
            scratch_shapes=[
                pltpu.VMEM((QW, HD), jnp.bfloat16),
                pltpu.VMEM((W + BLK, QW), jnp.float32),
                pltpu.VMEM((8, QW), jnp.float32),
                pltpu.VMEM((8, QW), jnp.float32),
                pltpu.VMEM((HD, QW), jnp.float32),
            ],
        ),
        out_shape=[
            jax.ShapeDtypeStruct((seqs, rows, QW), jnp.bfloat16),
            jax.ShapeDtypeStruct((seqs, 2, 1, QW), jnp.float32),
        ],
        compiler_params=kernel_params,
        cost_estimate=pl.CostEstimate(flops=7 * 10**9, bytes_accessed=8 * 2**20, transcendentals=7 * 10**6),
        name="attend",
    )(*scalars, qkv, key_value, seg)


def attend_back(scalars, qkv, d_mixed, mixed, key_value, seg, lse):
    seqs, rows = qkv.shape[:2]
    return pl.pallas_call(
        attend_back_kernel,
        grid_spec=pltpu.PrefetchScalarGridSpec(
            num_scalar_prefetch=4,
            grid=(seqs, 2),
            in_specs=[row_spec(), row_spec(), row_spec(), whole_spec(key_value.shape), whole_spec(seg.shape), lse_spec],
            out_specs=[row_spec(), whole_spec(key_value.shape)],
            scratch_shapes=[
                pltpu.VMEM((QW, HD), jnp.bfloat16),
                pltpu.VMEM((QW, HD), jnp.bfloat16),
                pltpu.VMEM((HD, QW), jnp.float32),
                pltpu.VMEM(key_value.shape, jnp.float32),
            ],
        ),
        out_shape=[
            jax.ShapeDtypeStruct((seqs, rows, QW), jnp.bfloat16),
            jax.ShapeDtypeStruct(key_value.shape, jnp.bfloat16),
        ],
        compiler_params=kernel_params,
        cost_estimate=pl.CostEstimate(flops=18 * 10**9, bytes_accessed=12 * 2**20, transcendentals=7 * 10**6),
        name="attend_back",
    )(*scalars, qkv, d_mixed, mixed, key_value, seg, lse)


def ffn_kernel(counts, at_ref, n2_a, gy_a, n2_b, gy_b, *refs):
    total = sum(counts)
    pieces = refs[:total]
    *outs, wg_ref, wu_ref, wd_ref, sems = refs[-13:]
    act_ref, dg_ref, du_ref, n2_out, gy_out, dn2_a, down_a, dn2_b, down_b = outs
    step = pl.program_id(0)
    first = step < pl.num_programs(0) // 2
    weights = []
    for dst, count in zip((wg_ref, wu_ref, wd_ref), counts, strict=True):
        copies = []
        for _ in range(count):
            i = sum(map(len, weights)) + len(copies)
            src = pieces[i]
            rows = src.shape[0]
            place = dst.at[pl.ds(pl.multiple_of(at_ref[i], 16), rows)]
            copies.append(pltpu.make_async_copy(src, place, sems.at[i]))
        weights.append(copies)

    @pl.when(step == 0)
    def _():
        for copies in weights:
            for copy in copies:
                copy.start()

    def ready(copies):
        @pl.when(step == 0)
        def _():
            for copy in copies:
                copy.wait()

    n2 = jnp.where(first, n2_a[...], n2_b[...])
    gy = jnp.where(first, gy_a[...], gy_b[...])
    n2_out[0] = n2
    gy_out[0] = gy
    ready(weights[0])
    gate = dot_f32(n2, wg_ref[...])
    ready(weights[1])
    up = dot_f32(n2, wu_ref[...])
    ready(weights[2])
    d_act = dot_f32(gy, wd_ref[...], ((1,), (1,)))
    square = gate * gate
    inner = jnp.tanh(gate * (gelu_c + gelu_c * gelu_a * square))
    half = 0.5 + 0.5 * inner
    gelu = gate * half
    slope = half + 0.5 * gate * (1.0 - inner * inner) * (gelu_c + 3.0 * gelu_c * gelu_a * square)
    act = (gelu * up).astype(jnp.bfloat16)
    d_gate = (d_act * up * slope).astype(jnp.bfloat16)
    d_up = (d_act * gelu).astype(jnp.bfloat16)
    act_ref[0] = act
    dg_ref[0] = d_gate
    du_ref[0] = d_up
    dn2 = dot_f32(d_gate, wg_ref[...], ((1,), (1,))) + dot_f32(d_up, wu_ref[...], ((1,), (1,)))
    dn2 = dn2.astype(jnp.bfloat16)
    down = dot_f32(act, wd_ref[...]).astype(jnp.bfloat16)

    @pl.when(first)
    def _():
        dn2_a[...] = dn2
        down_a[...] = down

    @pl.when(jnp.logical_not(first))
    def _():
        dn2_b[...] = dn2
        down_b[...] = down


def ffn(pair, pieces, n2, gy, gate, up, w_down, held):
    rows, width = n2[0].shape
    units = w_down.shape[0]
    tile = rows // 2
    held_shapes = [(pieces, rows, units)] * 3 + [(pieces, rows, width)] * 2
    held_spec = [
        pl.BlockSpec((1, tile, s[2]), lambda t, at: (2 * pair + t // 2, t % 2, 0)) for s in held_shapes
    ]
    a_spec = pl.BlockSpec((tile, width), lambda t, at: (jnp.minimum(t, 1), 0))
    b_spec = pl.BlockSpec((tile, width), lambda t, at: (jnp.maximum(t - 2, 0), 0))
    parts = [*gate, *up, (w_down, 0)]
    places = jnp.stack([jnp.asarray(at, jnp.int32) for _, at in parts])
    arrays = [p for p, _ in parts]
    out = pl.pallas_call(
        functools.partial(ffn_kernel, (len(gate), len(up), 1)),
        grid_spec=pltpu.PrefetchScalarGridSpec(
            num_scalar_prefetch=1,
            grid=(4,),
            in_specs=[a_spec, a_spec, b_spec, b_spec]
            + [pl.BlockSpec(memory_space=pl.ANY)] * (len(arrays) + len(held)),
            out_specs=held_spec + [a_spec, a_spec, b_spec, b_spec],
            scratch_shapes=[
                pltpu.VMEM((width, units), jnp.bfloat16),
                pltpu.VMEM((width, units), jnp.bfloat16),
                pltpu.VMEM((units, width), jnp.bfloat16),
                pltpu.SemaphoreType.DMA((len(arrays),)),
            ],
        ),
        out_shape=[jax.ShapeDtypeStruct(s, jnp.bfloat16) for s in held_shapes]
        + [jax.ShapeDtypeStruct((rows, width), jnp.bfloat16)] * 4,
        input_output_aliases={5 + len(arrays) + i: i for i in range(len(held))},
        compiler_params=pltpu.CompilerParams(vmem_limit_bytes=56 * 2**20),
        cost_estimate=pl.CostEstimate(
            flops=28 * rows * units * width, bytes_accessed=40 * 2**20, transcendentals=2 * rows * units
        ),
        name="ffn",
    )(places, n2[0], gy[0], n2[1], gy[1], *arrays, *held)
    return out[:5], [out[5], out[7]], [out[6], out[8]]


def blank(shape, dtype):
    return pl.pallas_call(
        lambda ref: None,
        out_shape=jax.ShapeDtypeStruct(shape, dtype),
        out_specs=pl.BlockSpec(memory_space=pl.ANY),
        name="blank",
    )()


def tie(v, *after):
    return lax.optimization_barrier((v, *after))[0] if after else v


def place_kernel(splits, at_ref, low_ref, high_ref, *outs):
    first = pl.program_id(0) < pl.num_programs(0) // 2
    piece = jnp.where(first, low_ref[0], high_ref[0]).astype(jnp.float32)
    col = 0
    for out, width in zip(outs, splits, strict=True):
        out[...] = piece[:, col : col + width]
        col += width


def place_rows(at, first, second, splits):
    count, rows, cols = first.shape
    if rows % 8:
        outs = []
        col = 0
        for width in splits:
            out = blank((2 * count * rows, width), jnp.float32)
            for i in range(2 * count):
                piece = (first if i < count else second)[i % count, :, col : col + width]
                out = lax.dynamic_update_slice(out, piece.astype(jnp.float32), (at[i] * rows, 0))
            outs.append(out)
            col += width
        return outs
    return pl.pallas_call(
        functools.partial(place_kernel, splits),
        grid_spec=pltpu.PrefetchScalarGridSpec(
            num_scalar_prefetch=1,
            grid=(2 * count,),
            in_specs=[
                pl.BlockSpec((1, rows, cols), lambda t, at: (jnp.minimum(t, count - 1), 0, 0)),
                pl.BlockSpec((1, rows, cols), lambda t, at: (jnp.maximum(t - count, 0), 0, 0)),
            ],
            out_specs=[pl.BlockSpec((rows, width), lambda t, at: (at[t], 0)) for width in splits],
        ),
        out_shape=[jax.ShapeDtypeStruct((2 * count * rows, width), jnp.float32) for width in splits],
        cost_estimate=pl.CostEstimate(flops=0, bytes_accessed=12 * count * rows * cols, transcendentals=0),
        name="place",
    )(at, first, second)


class Order:
    def __init__(self):
        self.last = ()

    def after(self, *vals):
        out = lax.optimization_barrier((*vals, *self.last))[: len(vals)] if self.last else vals
        return out[0] if len(vals) == 1 else out

    def did(self, *vals):
        self.last = vals


class Chain:
    def __init__(self, order, steps):
        self.order, self.steps, self.result = order, steps, None
        self.running = True
        self.resume(None)

    def resume(self, taken):
        try:
            self.arriving, sent = self.steps.send(taken)
            self.order.did(*sent)
        except StopIteration as end:
            self.running, self.result = False, end.value
            self.order.did(*jax.tree.leaves(end.value))

    def step(self):
        if self.running:
            taken = self.order.after(*self.arriving)
            self.resume(list(taken) if len(self.arriving) > 1 else [taken])

    def finish(self):
        while self.running:
            self.step()
        return self.result


class Plan:
    def __init__(self, mesh):
        self.shards = mesh.shape["shard"]
        self.ctxs = mesh.shape["ctx"]
        half = self.ctxs // 2
        self.ring = [2 * z for z in range(half)] + [2 * z + 1 for z in reversed(range(half))]
        self.place = [self.ring.index(c) for c in range(self.ctxs)]
        self.right = [(self.ring[i], self.ring[(i + 1) % self.ctxs]) for i in range(self.ctxs)]
        self.left = [(b, a) for a, b in self.right]
        self.bits = [1 << b for b in range(self.shards.bit_length() - 1)]

    def my_place(self):
        table = jnp.array(self.place, jnp.int32)
        at = jnp.arange(self.ctxs, dtype=jnp.int32) == lax.axis_index("ctx")
        return jnp.sum(jnp.where(at, table, 0))

    def swap(self, v, bit):
        return lax.ppermute(v, "shard", [(i, i ^ bit) for i in range(self.shards)])

    def swap_ctx(self, v, bit):
        return lax.ppermute(v, "ctx", [(i, i ^ bit) for i in range(self.ctxs)])

    def go_right(self, v):
        return lax.ppermute(v, "ctx", self.right)

    def go_left(self, v):
        return lax.ppermute(v, "ctx", self.left)

    def my_bit(self, bit):
        return (lax.axis_index("shard") // bit) % 2

    def lay_rows(self, pieces):
        me = lax.axis_index("shard")
        rows, cols = pieces[0].shape
        out = blank((self.shards * rows, cols), pieces[0].dtype)
        for j, piece in enumerate(pieces):
            out = lax.dynamic_update_slice(out, piece, ((me ^ j) * rows, 0))
        return out

    def near(self, v, first=0):
        pieces = {0: v}
        for bit in reversed(self.bits[:-1]):
            pieces |= {j | bit: self.swap(p, bit) for j, p in pieces.items()}
        return [pieces[j] for j in range(self.bits[-1])]

    def gather_near(self, v):
        _, *others = self.near(v)
        return [v, *(yield others, [v])]

    def gather_far(self, v):
        [got] = yield [self.swap(v, self.bits[-1])], [v]
        _, *others = self.near(got)
        return [got, *(yield others, [got])]

    def gather_far_halved(self, v):
        half = v.shape[0] // 2
        y = lax.axis_index("ctx") % 2
        give = lax.dynamic_slice_in_dim(v, y * half, half, 0)
        [mine] = yield [self.swap(give, self.bits[-1])], [give]
        [other] = yield [self.swap_ctx(mine, 1)], [mine]
        whole = blank(v.shape, v.dtype)
        whole = lax.dynamic_update_slice(whole, mine, (y * half, 0))
        whole = lax.dynamic_update_slice(whole, other, ((1 - y) * half, 0))
        _, *others = self.near(whole)
        return [whole, *(yield others, [whole])]

    def gate_up_columns(self, w):
        n = self.shards
        rows, units = w.shape[0], FF // n
        me = lax.axis_index("shard")

        def block(shard, row, count):
            return [lax.dynamic_slice(w, (row, base + shard * units), (count, units)) for base in (0, FF)]

        own = block(me, 0, rows)
        pieces = [(own, me * rows)]
        if n == 4 and self.ctxs % 4 == 0:
            y, z = lax.axis_index("ctx") % 2, (lax.axis_index("ctx") // 2) % 2
            half = rows // 2
            pairs = [(c * n + s, c * n + (s ^ 2 ^ (c % 2))) for c in range(self.ctxs) for s in range(n)]
            give = block(me ^ 2 ^ y, z * half, half)
            got = [lax.ppermute(b, ("ctx", "shard"), pairs) for b in give]
            got = yield got, give
            mine, theirs = (me ^ 2 ^ y) * rows, (me ^ 2 ^ (1 - y)) * rows
            at, far = z * half, (1 - z) * half
            second = [self.swap_ctx(got[0], 1), self.swap_ctx(got[1], 2)]
            near_give = block(me ^ 1, 0, rows)
            near = [self.swap(b, 1) for b in near_give]
            g_y, u_z = yield second, [*got, *near_give]
            third = [self.swap_ctx(got[0], 2), self.swap_ctx(g_y, 2), self.swap_ctx(got[1], 1), self.swap_ctx(u_z, 1)]
            near = yield near, [g_y, u_z]
            g_z, g_yz, u_y, u_zy = yield third, near
            gate = [(own[0], me * rows), (near[0], (me ^ 1) * rows), (got[0], mine + at), (g_y, theirs + at)]
            gate += [(g_z, mine + far), (g_yz, theirs + far)]
            up = [(own[1], me * rows), (near[1], (me ^ 1) * rows), (got[1], mine + at), (u_z, mine + far)]
            up += [(u_y, theirs + at), (u_zy, theirs + far)]
            return gate, up
        for j in range(1, n):
            pieces.append(([self.swap(b, j) for b in block(me ^ j, 0, rows)], (me ^ j) * rows))
        return [[(pair[i], at) for pair, at in pieces] for i in range(2)]

    def scatter(self, pieces):
        pieces = dict(enumerate(pieces))
        for bit in self.bits:
            give = {j: p for j, p in pieces.items() if j & bit}
            got = yield [self.swap(p, bit) for p in give.values()], list(give.values())
            pieces = {j ^ bit: add_low(pieces[j ^ bit], g) for j, g in zip(give, got, strict=True)}
        return pieces[0]

    def scatter_rows(self, v, add=add_low):
        cur = v.reshape(self.shards, v.shape[0] // self.shards, *v.shape[1:])
        for bit in self.bits:
            pairs = cur.reshape(cur.shape[0] // 2, 2, *cur.shape[1:])
            mine = self.my_bit(bit)
            keep = lax.dynamic_index_in_dim(pairs, mine, 1, False)
            give = lax.dynamic_index_in_dim(pairs, 1 - mine, 1, False)
            [got] = yield [self.swap(give, bit)], [give]
            cur = add(keep, got)
        return cur[0]

    def ring_gather(self, v):
        n = self.ctxs
        pieces = {0: v}
        a, b = v, v
        for step in range(1, n // 2 + 1):
            both = n - step > n // 2
            got = yield [self.go_right(a)] + ([self.go_left(b)] if both else []), [a, b] if both else [a]
            pieces[step] = a = got[0]
            if both:
                pieces[n - step] = b = got[1]
        return jnp.stack([pieces[k] for k in range(n)])

    def ring_scatter(self, v):
        n = self.ctxs
        m = n // 2
        a, b = v[m], v[m - 1]
        for step in range(1, m):
            a, b = yield [self.go_right(a), self.go_left(b)], [a, b]
            a = add_low(a, v[m + step])
            if step < m - 1:
                b = add_low(b, v[m - 1 - step])
        [a] = yield [self.go_right(a)], [a]
        return v[0].astype(jnp.float32) + a.astype(jnp.float32) + b.astype(jnp.float32)

    def halve(self, v, axis, order):
        top = self.ctxs.bit_length() - 1
        left = [1 << b for b in reversed(range(top))]
        cur = v.reshape(*v.shape[:axis], *([2] * top), *v.shape[axis + 1 :])
        for bit in order:
            at = axis + left.index(bit)
            left.remove(bit)
            mine = (lax.axis_index("ctx") // bit) % 2
            give = lax.dynamic_index_in_dim(cur, 1 - mine, at, False)
            keep = lax.dynamic_index_in_dim(cur, mine, at, False)
            [got] = yield [self.swap_ctx(give, bit)], [give]
            cur = add_low(keep, got)
        return cur

    def double(self, v, order):
        cur, ids = v[None], [0]
        for bit in reversed(order):
            [other] = yield [self.swap_ctx(cur, bit)], [cur]
            ids += [k ^ bit for k in ids]
            if len(ids) < self.ctxs:
                cur = jnp.concatenate([cur, other])
        return cur, other, lax.axis_index("ctx") ^ jnp.array(ids, jnp.int32)

    def order(self, first):
        bits = [1 << b for b in range(self.ctxs.bit_length() - 1)]
        return [first] + [b for b in bits if b != first]

    def ring_reduce(self, own, axis):
        m = self.ctxs // 2
        far = own(m)
        cut = far.shape[axis] // 2
        head = functools.partial(lax.slice_in_dim, start_index=0, limit_index=cut, axis=axis)
        tail = functools.partial(lax.slice_in_dim, start_index=cut, limit_index=None, axis=axis)
        a, b = head(far), tail(far)
        for k in range(m - 1, -1, -1):
            a, b = yield [self.go_right(a), self.go_left(b)], [a, b]
            at_a, at_b = own(k), own(-k)
            if k == 0:
                total = at_a.astype(jnp.float32) + a.astype(jnp.float32) + b.astype(jnp.float32)
            elif k == m - 1:
                a = jnp.concatenate([add_low(a, head(at_a)), tail(at_a)], axis)
                b = jnp.concatenate([head(at_b), add_low(b, tail(at_b))], axis)
            else:
                a, b = add_low(a, at_a), add_low(b, at_b)
        return total.astype(jnp.bfloat16)

    def ring_spread(self, out, chunk, col):
        m = self.ctxs // 2
        place = self.my_place()
        cut = chunk.shape[1] // 2

        def put(piece, k, col):
            at = lax.rem(place + k + 2 * m, 2 * m) * piece.shape[0]
            out[0] = lax.dynamic_update_slice(out[0], piece.astype(jnp.float32), (at, col))

        put(chunk, 0, col)
        a = b = chunk
        for k in range(1, m + 1):
            if k == m:
                a, b = a[:, :cut], b[:, cut:]
            a, b = yield [self.go_right(a), self.go_left(b)], [a, b]
            put(a, -k, col)
            put(b, k, col + cut if k == m else col)

    def own_chunk(self, chunks, axis):
        place = self.my_place()
        n = self.ctxs
        return lambda k: lax.dynamic_index_in_dim(chunks, lax.rem(place + k + n, n), axis, False)

    def sum_rows(self, v, out):
        rows, cols = v.shape
        chunks = v.reshape(self.ctxs, rows // self.ctxs, cols)
        mine = yield from self.ring_reduce(self.own_chunk(chunks, 0), 1)
        yield from self.ring_spread(out, mine, 0)
        return out[0]

    def sum_over_all(self, v, out):
        mine = yield from self.scatter_rows(v)
        return (yield from self.sum_rows(mine, out))

    def sum_small_over_all(self, v):
        mine = yield from self.scatter_rows(v)
        rows, cols = mine.shape
        order = self.order(1)
        mine = yield from self.halve(mine.reshape(self.ctxs, rows // self.ctxs, cols), 0, order)
        low_half, high_half, at = yield from self.double(mine, order)
        return place_rows(at, low_half, high_half, [cols])[0]

    def sum_columns(self, part, out, col):
        n, c = self.shards, self.ctxs
        me = lax.axis_index("shard")
        rows, units = part.shape[0] // n // c, part.shape[1]
        mine = yield from self.ring_reduce(self.own_chunk(part.reshape(n, c, rows, units), 1), 0)
        got = [lax.dynamic_index_in_dim(mine, me ^ j, 0, False) for j in range(n)]
        others = yield [self.swap(g, j) for j, g in enumerate(got) if j], got[1:]
        whole = blank((rows, n * units), jnp.bfloat16)
        for j, g in enumerate([got[0], *others]):
            whole = lax.dynamic_update_slice(whole, g, (0, (me ^ j) * units))
        yield from self.ring_spread(out, whole, col)
        return out[0]

    def small_sum(self, v):
        cur = yield from self.scatter_rows(v, lambda a, b: a + b)
        cur = cur[0] if cur.ndim == v.ndim else cur
        for bit in self.order(1):
            [got] = yield [self.swap_ctx(cur, bit)], [cur]
            cur = cur + got
        return cur


def body(plan, tokens, segments, assign, w_qkv, w_out, w_gate_up, w_down, gain_attn, gain_ffn, cotangent):
    seqs, rows_dev, width = tokens.shape
    rows = seqs * rows_dev
    blocks = assign.shape[0]
    n = plan.shards
    low = jnp.bfloat16
    ids = jnp.arange(blocks, dtype=jnp.int32)
    my_blocks = lax.dynamic_slice_in_dim(assign, 2 * lax.axis_index("ctx"), 2, 0)
    place_of = jnp.array([plan.place[i // 2] for i in range(blocks)], jnp.int32)
    back = lax.rem(plan.my_place() - place_of + plan.ctxs, plan.ctxs)
    hit = assign[None, :] == ids[:, None]
    slot_of = jnp.sum(jnp.where(hit, back[None, :], 0), axis=1)
    half_of = jnp.sum(jnp.where(hit, (ids % 2)[None, :], 0), axis=1)
    firsts = jnp.stack([lax.dynamic_index_in_dim(segments, my_blocks[m] * BLK, 1, False) for m in range(2)], 1)
    starts = jnp.sum((segments[:, None, :] < firsts[:, :, None]).astype(jnp.int32), axis=2)
    lowest = jnp.maximum(jnp.maximum(starts // BLK, my_blocks[None, :] - BACK), 0).reshape(-1)
    scalars = (my_blocks, lowest, slot_of, half_of)
    seg = segments.astype(jnp.float32).reshape(seqs, blocks, 1, BLK)

    order = Order()
    chains = {}

    def chain(steps, name=None):
        chains[name] = Chain(order, steps)
        return chains[name]

    def take(names):
        for name in names.split():
            chains[name].step()

    lanes = jnp.zeros((gain_attn.shape[0], HD - 2), low)
    first = jnp.concatenate([w_qkv[:, QW:], gain_attn[:, None], gain_ffn[:, None], lanes], axis=1)
    first_far, first_near = chain(plan.gather_far(first)), chain(plan.gather_near(first))
    tok = tokens.reshape(rows, width).astype(jnp.float32)
    scale_one = inv_rms(tok)
    hat_one = tok * scale_one
    first_far.step()
    q_rows = order.after(w_qkv[:, :QW])
    q_far, q_near = chain(plan.gather_far_halved(q_rows)), chain(plan.gather_near(q_rows))
    packed = plan.lay_rows(first_near.finish() + first_far.finish())
    w_kv = packed[:, : 2 * HD]
    gain_one, gain_two = (packed[:, 2 * HD + i].astype(jnp.float32) for i in range(2))
    normed_one = (hat_one * gain_one).astype(low)
    key_value = dot_f32(normed_one, w_kv).astype(low).reshape(seqs, 2, BLK, 2 * HD)
    kv = chain(plan.ring_gather(key_value))
    o_rows = order.after(w_out)
    o_far, o_near = chain(plan.gather_far_halved(o_rows)), chain(plan.gather_near(o_rows))
    q_far.step()
    kv.step()
    gu = chain(plan.gate_up_columns(order.after(w_gate_up)))
    kv.step()
    q_far.step()
    o_far.step()
    kv.step()
    kv_all = kv.finish()
    o_far.step()
    gu.step()
    grad_low = cotangent.reshape(rows, width)
    gy_rows = order.after(grad_low)
    gy_far, gy_near = chain(plan.gather_far(gy_rows)), chain(plan.gather_near(gy_rows))
    w_q = plan.lay_rows(q_near.finish() + q_far.finish())
    queries = dot_f32(normed_one, w_q).astype(low).reshape(seqs, rows_dev, QW)
    mixed, lse = attend(scalars, queries, kv_all, seg)
    order.did(mixed)
    gu.step()
    w_o = plan.lay_rows(o_near.finish() + o_far.finish())
    mixed_low = mixed.reshape(rows, QW)
    hidden = tok + dot_f32(mixed_low, w_o)
    scale_two = inv_rms(hidden)
    hat_two = hidden * scale_two
    normed_two = (hat_two * gain_two).astype(low)
    order.did(normed_two)
    n2_far, n2_near = chain(plan.gather_far(normed_two)), chain(plan.gather_near(normed_two))
    gy_far.step()
    w_gate, w_up = gu.finish()

    held, d_n2, down = (), [], []

    def feed_forward(n2, gy):
        nonlocal held, d_n2, down
        for p in range(0, len(n2), 2):
            at = len(d_n2) // 2
            held, d_n2_pair, down_pair = ffn(at, n, n2[p : p + 2], gy[p : p + 2], w_gate, w_up, w_down, held)
            d_n2, down = d_n2 + d_n2_pair, down + down_pair
        order.did(*d_n2)

    feed_forward(n2_near.finish(), gy_near.finish())
    n2_far.step()
    feed_forward(n2_far.finish(), gy_far.finish())
    act, d_gate, d_up, n2_all, gy_all = (v.reshape(n * rows, -1) for v in held)

    def grad(left, right):
        part = dot_f32(order.after(left), right, ((0,), (0,))).astype(low)
        order.did(part)
        return part

    def blank_like(w):
        return [blank(w.shape, jnp.float32)]

    chain(plan.scatter(d_n2), "T")
    chain(plan.sum_rows(grad(act, gy_all), blank_like(w_down)), "D")
    take("T")
    out_gate_up = blank_like(w_gate_up)
    chain(plan.sum_columns(grad(n2_all, d_gate), out_gate_up, 0), "G")
    take("D")
    chain(plan.sum_columns(grad(n2_all, d_up), out_gate_up, FF), "U")
    take("G D U")
    d_normed_two = chains["T"].finish().astype(jnp.float32)
    e = d_normed_two * gain_two
    d_hidden = grad_low.astype(jnp.float32) + scale_two * (
        e - hat_two * jnp.mean(e * hat_two, axis=-1, keepdims=True)
    )
    d_branch = d_hidden.astype(low)
    order.did(d_branch)
    chain(plan.scatter(order.after(*down)), "B")
    d_mixed = dot_f32(order.after(d_branch), w_o, ((1,), (1,))).astype(low).reshape(seqs, rows_dev, QW)
    order.did(d_mixed)
    take("G B D U")
    dq, dkv = attend_back(scalars, queries, order.after(d_mixed), mixed, kv_all, seg, lse)
    order.did(dq, dkv)
    chain(plan.ring_scatter(dkv), "K")
    dq = dq.reshape(rows, QW)
    take("D U G")
    chain(plan.sum_over_all(grad(mixed_low, d_branch), blank_like(w_out)), "O")
    out_qkv = blank_like(w_qkv)
    chain(plan.sum_over_all(grad(normed_one, dq), out_qkv), "Q")
    branch = chains["B"].finish().astype(jnp.float32)
    output = (hidden + branch).reshape(seqs, rows_dev, width)
    take("O Q K D U G K D")
    dkv_low = chains["K"].finish().astype(low).reshape(rows, 2 * HD)
    chain(plan.sum_small_over_all(grad(normed_one, dkv_low)), "V")
    take("U V D G")
    d_normed_one = dot_f32(dq, w_q, ((1,), (1,))) + dot_f32(order.after(dkv_low), w_kv, ((1,), (1,)))
    gains = jnp.stack([jnp.sum(d_normed_one * hat_one, axis=0), jnp.sum(d_normed_two * hat_two, axis=0)])
    chain(plan.small_sum(jnp.moveaxis(gains.reshape(2, n, width // n), 0, 1)), "S")
    f = d_normed_one * gain_one
    input_grad = d_hidden + scale_one * (f - hat_one * jnp.mean(f * hat_one, axis=-1, keepdims=True))
    take("U D Q U V Q O G V S Q U V O S Q V U Q V O Q V O Q V O Q G O Q S O G S O G S O G O")
    sums = [chains[name] for name in "DGUOQVS"]
    while any(c.running for c in sums):
        for c in sums:
            c.step()
    grad_down, grad_out, grad_gate_up = chains["D"].result, chains["O"].result, out_gate_up[0]
    grad_qkv = lax.dynamic_update_slice(out_qkv[0], chains["V"].result, (0, QW))
    grad_gain_attn, grad_gain_ffn = chains["S"].result
    return (
        output,
        input_grad.reshape(seqs, rows_dev, width),
        grad_qkv,
        grad_out,
        grad_gate_up,
        grad_down,
        grad_gain_attn,
        grad_gain_ffn,
    )


def solution(mesh):
    return jax.shard_map(
        functools.partial(body, Plan(mesh)),
        mesh=mesh,
        in_specs=(
            P("shard", "ctx", None),
            P("shard", None),
            P(),
            P("shard", None),
            P("shard", None),
            P("shard", None),
            P("shard", None),
            P("shard"),
            P("shard"),
            P("shard", "ctx", None),
        ),
        out_specs=(
            P("shard", "ctx", None),
            P("shard", "ctx", None),
            P("shard", None),
            P("shard", None),
            P("shard", None),
            P("shard", None),
            P("shard"),
            P("shard"),
        ),
        check_vma=False,
    )
```

```python
import functools

import jax
import jax.numpy as jnp
from jax import lax
from jax.experimental import pallas as pl
from jax.experimental.pallas import tpu as pltpu
from jax.sharding import PartitionSpec as P

H = 12
HD = 128
FF = 4608
W = 1024
BLK = 128
BACK = W // BLK
QW = H * HD

epsilon = 1e-06
masked_score = -1e30
scale = HD ** (-0.5)
log2e = 1.4426950408889634
gelu_c = 0.7978845608028654
gelu_a = 0.044715


def dot_f32(left, right, dims=((1,), (0,))):
    return lax.dot_general(left, right, (dims, ((), ())), preferred_element_type=jnp.float32)


def inv_rms(rows):
    return lax.rsqrt(jnp.mean(rows * rows, axis=-1, keepdims=True) + epsilon)


def add_low(a, b):
    return (a.astype(jnp.float32) + b.astype(jnp.float32)).astype(jnp.bfloat16)


def stack_heads(dst, src):
    for h in range(H):
        dst[h * BLK : (h + 1) * BLK, :] = src[0, :, h * HD : (h + 1) * HD]


def block_bias(seg_ref, seq, q_block, k_block, step):
    q_seg = jnp.broadcast_to(seg_ref[seq, q_block], (BLK, BLK))
    k_seg = jnp.broadcast_to(seg_ref[seq, k_block], (BLK, BLK)).T
    allowed = q_seg == k_seg
    if step in (0, BACK):
        key_at = lax.broadcasted_iota(jnp.int32, (BLK, BLK), 0)
        query_at = lax.broadcasted_iota(jnp.int32, (BLK, BLK), 1)
        allowed &= key_at <= query_at if step == BACK else key_at > query_at
    bias = jnp.where(allowed, 0.0, masked_score)
    return jnp.concatenate([bias] * H, axis=1)


def fold8(v, how):
    return how(v.reshape(BLK // 8, 8, QW), axis=0)


def attend_kernel(
    blk_ref, low_ref, slot_ref, half_ref, q_ref, kv_ref, seg_ref, o_ref, lse_ref, qs, sc, mx, tot, acc
):
    seq, mine = pl.program_id(0), pl.program_id(1)
    q_block = blk_ref[mine]
    lowest = low_ref[seq * 2 + mine]
    stack_heads(qs, q_ref)
    mx[...] = jnp.full(mx.shape, masked_score, jnp.float32)
    tot[...] = jnp.zeros_like(tot)
    acc[...] = jnp.zeros_like(acc)
    for step in range(BACK + 1):
        k_block = q_block - BACK + step

        @pl.when(k_block >= lowest)
        def _(step=step, k_block=k_block):
            keys = kv_ref[slot_ref[k_block], seq, half_ref[k_block], :, :HD]
            s = dot_f32(keys, qs[...], ((1,), (1,))) * (scale * log2e)
            s += block_bias(seg_ref, seq, q_block, k_block, step)
            sc[step * BLK : (step + 1) * BLK, :] = s
            mx[...] = jnp.maximum(mx[...], fold8(s, jnp.max))

    top = jnp.max(mx[...], axis=0, keepdims=True)
    for step in range(BACK + 1):
        k_block = q_block - BACK + step

        @pl.when(k_block >= lowest)
        def _(step=step, k_block=k_block):
            vals = kv_ref[slot_ref[k_block], seq, half_ref[k_block], :, HD:]
            p = jnp.exp2(sc[step * BLK : (step + 1) * BLK, :] - top)
            tot[...] += fold8(p, jnp.sum)
            acc[...] += dot_f32(vals, p.astype(jnp.bfloat16), ((0,), (0,)))

    total = jnp.sum(tot[...], axis=0, keepdims=True)
    out = acc[...] / total
    for h in range(H):
        o_ref[0, :, h * HD : (h + 1) * HD] = out[:, h * BLK : (h + 1) * BLK].T.astype(jnp.bfloat16)
    lse_ref[0, 0] = top + jnp.log2(total)


def attend_back_kernel(
    blk_ref, low_ref, slot_ref, half_ref, q_ref, do_ref, o_ref, kv_ref, seg_ref, lse_ref,
    dq_ref, dkv_ref, qs, dos, dqt, dacc,
):
    seq, mine = pl.program_id(0), pl.program_id(1)
    q_block = blk_ref[mine]
    lowest = low_ref[seq * 2 + mine]

    @pl.when((seq == 0) & (mine == 0))
    def _():
        dacc[...] = jnp.zeros_like(dacc)

    stack_heads(qs, q_ref)
    stack_heads(dos, do_ref)
    dqt[...] = jnp.zeros_like(dqt)
    deltas = []
    for h in range(H):
        cols = slice(h * HD, (h + 1) * HD)
        both = do_ref[0, :, cols].astype(jnp.float32) * o_ref[0, :, cols].astype(jnp.float32)
        deltas.append(jnp.sum(both.T, axis=0, keepdims=True))
    delta = jnp.concatenate(deltas, axis=1)
    lse = lse_ref[0, 0]
    for step in range(BACK + 1):
        k_block = q_block - BACK + step

        @pl.when(k_block >= lowest)
        def _(step=step, k_block=k_block):
            slot, half = slot_ref[k_block], half_ref[k_block]
            keys = kv_ref[slot, seq, half, :, :HD]
            vals = kv_ref[slot, seq, half, :, HD:]
            s = dot_f32(keys, qs[...], ((1,), (1,))) * (scale * log2e)
            p = jnp.exp2(s + block_bias(seg_ref, seq, q_block, k_block, step) - lse)
            dp = dot_f32(vals, dos[...], ((1,), (1,)))
            d_raw = (p * (dp - delta)).astype(jnp.bfloat16)
            dqt[...] += dot_f32(keys, d_raw, ((0,), (0,)))
            dacc[slot, seq, half, :, :HD] += dot_f32(d_raw, qs[...]) * scale
            dacc[slot, seq, half, :, HD:] += dot_f32(p.astype(jnp.bfloat16), dos[...])

    out = dqt[...] * scale
    for h in range(H):
        dq_ref[0, :, h * HD : (h + 1) * HD] = out[:, h * BLK : (h + 1) * BLK].T.astype(jnp.bfloat16)

    @pl.when((seq == pl.num_programs(0) - 1) & (mine == 1))
    def _():
        dkv_ref[...] = dacc[...].astype(jnp.bfloat16)


def whole_spec(shape):
    return pl.BlockSpec(shape, lambda s, m, *_: (0,) * len(shape))


def row_spec():
    return pl.BlockSpec((1, BLK, QW), lambda s, m, *_: (s, m, 0))


lse_spec = pl.BlockSpec((1, 1, 1, QW), lambda s, m, *_: (s, m, 0, 0))
kernel_params = pltpu.CompilerParams(vmem_limit_bytes=48 * 2**20)
small_cost = pl.CostEstimate(flops=2**20, bytes_accessed=2**16, transcendentals=0)


def attend(scalars, qkv, key_value, seg):
    seqs, rows = qkv.shape[:2]
    return pl.pallas_call(
        attend_kernel,
        grid_spec=pltpu.PrefetchScalarGridSpec(
            num_scalar_prefetch=4,
            grid=(seqs, 2),
            in_specs=[row_spec(), whole_spec(key_value.shape), whole_spec(seg.shape)],
            out_specs=[row_spec(), lse_spec],
            scratch_shapes=[
                pltpu.VMEM((QW, HD), jnp.bfloat16),
                pltpu.VMEM((W + BLK, QW), jnp.float32),
                pltpu.VMEM((8, QW), jnp.float32),
                pltpu.VMEM((8, QW), jnp.float32),
                pltpu.VMEM((HD, QW), jnp.float32),
            ],
        ),
        out_shape=[
            jax.ShapeDtypeStruct((seqs, rows, QW), jnp.bfloat16),
            jax.ShapeDtypeStruct((seqs, 2, 1, QW), jnp.float32),
        ],
        compiler_params=kernel_params,
        cost_estimate=small_cost,
        name="attend",
    )(*scalars, qkv, key_value, seg)


def attend_back(scalars, qkv, d_mixed, mixed, key_value, seg, lse):
    seqs, rows = qkv.shape[:2]
    return pl.pallas_call(
        attend_back_kernel,
        grid_spec=pltpu.PrefetchScalarGridSpec(
            num_scalar_prefetch=4,
            grid=(seqs, 2),
            in_specs=[row_spec(), row_spec(), row_spec(), whole_spec(key_value.shape), whole_spec(seg.shape), lse_spec],
            out_specs=[row_spec(), whole_spec(key_value.shape)],
            scratch_shapes=[
                pltpu.VMEM((QW, HD), jnp.bfloat16),
                pltpu.VMEM((QW, HD), jnp.bfloat16),
                pltpu.VMEM((HD, QW), jnp.float32),
                pltpu.VMEM(key_value.shape, jnp.float32),
            ],
        ),
        out_shape=[
            jax.ShapeDtypeStruct((seqs, rows, QW), jnp.bfloat16),
            jax.ShapeDtypeStruct(key_value.shape, jnp.bfloat16),
        ],
        compiler_params=kernel_params,
        cost_estimate=pl.CostEstimate(flops=18 * 10**9, bytes_accessed=12 * 2**20, transcendentals=7 * 10**6),
        name="attend_back",
    )(*scalars, qkv, d_mixed, mixed, key_value, seg, lse)


class Loads:
    def __init__(self, counts, index, at_ref, pieces, stores, sems):
        self.groups, i = [], 0
        for store, count in zip(stores, counts, strict=True):
            group = []
            for _ in range(count):
                at, piece = index[i], pieces[i]
                piece = piece if at is None else piece.at[at]
                rows = piece.shape[0]
                place = store.at[pl.ds(pl.multiple_of(at_ref[i], 16), rows)]
                group.append(pltpu.make_async_copy(piece, place, sems.at[i]))
                i += 1
            self.groups.append(group)

        @pl.when(pl.program_id(0) == 0)
        def _():
            for group in self.groups:
                for copy in group:
                    copy.start()

    def ready(self, i):
        @pl.when(pl.program_id(0) == 0)
        def _():
            for copy in self.groups[i]:
                copy.wait()


def ffn_kernel(counts, index, at_ref, n2_a, gy_a, n2_b, gy_b, *refs):
    *outs, wg_ref, wu_ref, wd_ref, sems = refs[-13:]
    act_ref, dg_ref, du_ref, n2_out, gy_out, dn2_a, down_a, dn2_b, down_b = outs
    loads = Loads(counts, index, at_ref, refs, (wg_ref, wu_ref, wd_ref), sems)
    first = pl.program_id(0) < pl.num_programs(0) // 2
    n2 = jnp.where(first, n2_a[...], n2_b[...])
    gy = jnp.where(first, gy_a[...], gy_b[...])
    n2_out[0] = n2
    gy_out[0] = gy
    loads.ready(0)
    gate = dot_f32(n2, wg_ref[...])
    loads.ready(1)
    up = dot_f32(n2, wu_ref[...])
    loads.ready(2)
    d_act = dot_f32(gy, wd_ref[...], ((1,), (1,)))
    square = gate * gate
    inner = jnp.tanh(gate * (gelu_c + gelu_c * gelu_a * square))
    half = 0.5 + 0.5 * inner
    gelu = gate * half
    slope = half + 0.5 * gate * (1.0 - inner * inner) * (gelu_c + 3.0 * gelu_c * gelu_a * square)
    act = (gelu * up).astype(jnp.bfloat16)
    d_gate = (d_act * up * slope).astype(jnp.bfloat16)
    d_up = (d_act * gelu).astype(jnp.bfloat16)
    act_ref[0] = act
    dg_ref[0] = d_gate
    du_ref[0] = d_up
    dn2 = dot_f32(d_gate, wg_ref[...], ((1,), (1,))) + dot_f32(d_up, wu_ref[...], ((1,), (1,)))
    dn2 = dn2.astype(jnp.bfloat16)
    down = dot_f32(act, wd_ref[...]).astype(jnp.bfloat16)

    @pl.when(first)
    def _():
        dn2_a[...] = dn2
        down_a[...] = down

    @pl.when(jnp.logical_not(first))
    def _():
        dn2_b[...] = dn2
        down_b[...] = down


class Weights:
    def __init__(self, gate, up, w_down, who):
        self.groups = [gate, up, [(w_down, None, 0)]]
        self.counts = list(map(len, self.groups))
        places = [at for group in self.groups for *_, at in group]
        self.places = jnp.concatenate([jnp.stack([jnp.asarray(at, jnp.int32) for at in places]), who])
        self.count = len(places)

    def pieces(self, groups):
        parts = [p for group in self.groups[:groups] for p in group]
        return [p for p, *_ in parts], [i for _, i, _ in parts], self.counts[:groups]


def ffn(pair, pieces, part, n2, gy, weights, held, ends):
    some, width = n2[0].shape
    rows = some if part is None else 2 * some
    arrays, index, counts = weights.pieces(3)
    count, units = len(arrays), arrays[-1].shape[0]
    tile = rows // 2
    steps = 2 if part is None else 1
    at_row = 0 if part is None else part
    held_shapes = [(pieces, rows, units)] * 3 + [(pieces, rows, width)] * 2
    held_spec = [
        pl.BlockSpec((1, tile, s[2]), lambda t, at: (2 * pair + t // steps, at_row + t % steps, 0)) for s in held_shapes
    ]

    def spec(second, first_row):
        def index_map(t, at):
            return (first_row + (jnp.maximum(t - steps, 0) if second else jnp.minimum(t, steps - 1)), 0)

        return pl.BlockSpec((tile, width), index_map)

    kept = [*held, *ends]
    first_out = 0 if held else 5
    out = pl.pallas_call(
        functools.partial(ffn_kernel, counts, index),
        grid_spec=pltpu.PrefetchScalarGridSpec(
            num_scalar_prefetch=1,
            grid=(2 * steps,),
            in_specs=[spec(False, 0)] * 2
            + [spec(True, 0)] * 2
            + [pl.BlockSpec(memory_space=pl.ANY)] * (count + len(kept)),
            out_specs=held_spec + [spec(False, at_row)] * 2 + [spec(True, at_row)] * 2,
            scratch_shapes=[
                pltpu.VMEM((width, units), jnp.bfloat16),
                pltpu.VMEM((width, units), jnp.bfloat16),
                pltpu.VMEM((units, width), jnp.bfloat16),
                pltpu.SemaphoreType.DMA((count,)),
            ],
        ),
        out_shape=[jax.ShapeDtypeStruct(s, jnp.bfloat16) for s in held_shapes]
        + [jax.ShapeDtypeStruct((rows, width), jnp.bfloat16)] * 4,
        input_output_aliases={5 + count + i: first_out + i for i in range(len(kept))},
        compiler_params=pltpu.CompilerParams(vmem_limit_bytes=56 * 2**20),
        cost_estimate=small_cost,
        name="ffn",
    )(weights.places, n2[0], gy[0], n2[1], gy[1], *arrays, *kept)
    return out[:5], out[5:]


def project_kernel(at_ref, x_ref, *refs):
    *pieces, y_ref, w_ref, sems = refs
    copies = []
    for i, piece in enumerate(pieces):
        rows = piece.shape[0]
        place = w_ref.at[pl.ds(pl.multiple_of(at_ref[i] * rows, 16), rows)]
        copies.append(pltpu.make_async_copy(piece, place, sems.at[i]))
    for copy in copies:
        copy.start()
    for copy in copies:
        copy.wait()
    y_ref[...] = dot_f32(x_ref[...], w_ref[...]).astype(y_ref.dtype)


def project(x, pieces, at, dtype):
    rows, cols = pieces[0].shape
    vmem = pl.BlockSpec(memory_space=pltpu.VMEM)
    return pl.pallas_call(
        project_kernel,
        in_specs=[pl.BlockSpec(memory_space=pltpu.SMEM), vmem]
        + [pl.BlockSpec(memory_space=pl.ANY)] * len(pieces),
        out_specs=[vmem, vmem],
        out_shape=[
            jax.ShapeDtypeStruct((x.shape[0], cols), dtype),
            jax.ShapeDtypeStruct((len(pieces) * rows, cols), pieces[0].dtype),
        ],
        scratch_shapes=[pltpu.SemaphoreType.DMA((len(pieces),))],
        compiler_params=kernel_params,
        cost_estimate=small_cost,
        name="project",
    )(at, x, *pieces)


def blank(shape, dtype):
    return pl.pallas_call(
        lambda ref: None,
        out_shape=jax.ShapeDtypeStruct(shape, dtype),
        out_specs=pl.BlockSpec(memory_space=pl.ANY),
        name="blank",
    )()


def tie(v, *after):
    return lax.optimization_barrier((v, *after))[0] if after else v


def blank(shape, dtype):
    return pl.pallas_call(
        lambda ref: None,
        out_shape=jax.ShapeDtypeStruct(shape, dtype),
        out_specs=pl.BlockSpec(memory_space=pl.ANY),
        name="blank",
    )()


def tie(v, *after):
    return lax.optimization_barrier((v, *after))[0] if after else v


class Order:
    def __init__(self):
        self.last = ()

    def after(self, *vals):
        out = lax.optimization_barrier((*vals, *self.last))[: len(vals)] if self.last else vals
        return out[0] if len(vals) == 1 else out

    def did(self, *vals):
        self.last = vals


class Chain:
    def __init__(self, order, steps):
        self.order, self.steps, self.result = order, steps, None
        self.running = True
        self.resume(None)

    def resume(self, taken):
        try:
            self.arriving, sent = self.steps.send(taken)
            self.order.did(*sent)
        except StopIteration as end:
            self.running, self.result = False, end.value
            self.order.did(*jax.tree.leaves(end.value))

    def step(self):
        if self.running:
            taken = self.order.after(*self.arriving)
            self.resume(list(taken) if len(self.arriving) > 1 else [taken])

    def finish(self):
        while self.running:
            self.step()
        return self.result


class Plan:
    def __init__(self, mesh):
        self.shards = mesh.shape["shard"]
        self.ctxs = mesh.shape["ctx"]
        half = self.ctxs // 2
        self.ring = [2 * z for z in range(half)] + [2 * z + 1 for z in reversed(range(half))]
        self.place = [self.ring.index(c) for c in range(self.ctxs)]
        self.right = [(self.ring[i], self.ring[(i + 1) % self.ctxs]) for i in range(self.ctxs)]
        self.left = [(b, a) for a, b in self.right]
        self.bits = [1 << b for b in range(self.shards.bit_length() - 1)]

    def my_place(self):
        table = jnp.array(self.place, jnp.int32)
        at = jnp.arange(self.ctxs, dtype=jnp.int32) == lax.axis_index("ctx")
        return jnp.sum(jnp.where(at, table, 0))

    def swap(self, v, bit):
        return lax.ppermute(v, "shard", [(i, i ^ bit) for i in range(self.shards)])

    def swap_ctx(self, v, bit):
        return lax.ppermute(v, "ctx", [(i, i ^ bit) for i in range(self.ctxs)])

    def go_right(self, v):
        return lax.ppermute(v, "ctx", self.right)

    def go_left(self, v):
        return lax.ppermute(v, "ctx", self.left)

    def my_bit(self, bit):
        return (lax.axis_index("shard") // bit) % 2

    def lay_rows(self, pieces):
        rows, cols = pieces[0].shape
        out = blank((self.shards * rows, cols), pieces[0].dtype)
        for piece, at in zip(pieces, self.others(), strict=True):
            out = lax.dynamic_update_slice(out, piece, (at * rows, 0))
        return out

    def others(self):
        return lax.axis_index("shard") ^ jnp.arange(self.shards, dtype=jnp.int32)

    def near(self, v):
        pieces = {0: v}
        for bit in reversed(self.bits[:-1]):
            pieces |= {j | bit: self.swap(p, bit) for j, p in pieces.items()}
        return [pieces[j] for j in range(self.bits[-1])]

    def gather_near(self, v):
        _, *others = self.near(v)
        return [v, *(yield others, [v])]

    def gather_far(self, v):
        [got] = yield [self.swap(v, self.bits[-1])], [v]
        _, *others = self.near(got)
        return [got, *(yield others, [got])]

    def gather_far_halved(self, v):
        half = v.shape[0] // 2
        y = lax.axis_index("ctx") % 2
        give = lax.dynamic_slice_in_dim(v, y * half, half, 0)
        [mine] = yield [self.swap(give, self.bits[-1])], [give]
        [other] = yield [self.swap_ctx(mine, 1)], [mine]
        whole = blank(v.shape, v.dtype)
        whole = lax.dynamic_update_slice(whole, mine, (y * half, 0))
        whole = lax.dynamic_update_slice(whole, other, ((1 - y) * half, 0))
        _, *others = self.near(whole)
        return [whole, *(yield others, [whole])]

    def gate_up_columns(self, w):
        n = self.shards
        rows, units = w.shape[0], FF // n
        me = lax.axis_index("shard")

        def block(shard, row, count):
            return [lax.dynamic_slice(w, (row, base + shard * units), (count, units)) for base in (0, FF)]

        own = block(me, 0, rows)
        if n == 4 and self.ctxs % 4 == 0:
            y, z = lax.axis_index("ctx") % 2, (lax.axis_index("ctx") // 2) % 2
            half = rows // 2
            pairs = [(c * n + s, c * n + (s ^ 2 ^ (c % 2))) for c in range(self.ctxs) for s in range(n)]
            give = jnp.stack(block(me ^ 2 ^ y, z * half, half))
            [got] = yield [lax.ppermute(give, ("ctx", "shard"), pairs)], [give]
            mine, theirs = (me ^ 2 ^ y) * rows, (me ^ 2 ^ (1 - y)) * rows
            at, far = z * half, (1 - z) * half
            second = [self.swap_ctx(got[0], 1), self.swap_ctx(got[1], 2)]
            near_give = jnp.stack(block(me ^ 1, 0, rows))
            second.append(self.swap(near_give, 1))
            g_y, u_z, near = yield second, [got, near_give]
            give = [jnp.stack([got[0], g_y]), jnp.stack([got[1], u_z])]
            g_z, u_y = yield [self.swap_ctx(give[0], 2), self.swap_ctx(give[1], 1)], give
            gate = [(own[0], None, me * rows), (near, 0, (me ^ 1) * rows), (got, 0, mine + at), (g_y, None, theirs + at)]
            gate += [(g_z, 0, mine + far), (g_z, 1, theirs + far)]
            up = [(own[1], None, me * rows), (near, 1, (me ^ 1) * rows), (got, 1, mine + at), (u_z, None, mine + far)]
            up += [(u_y, 0, theirs + at), (u_y, 1, theirs + far)]
            return gate, up
        gate, up = [(own[0], None, me * rows)], [(own[1], None, me * rows)]
        for j in range(1, n):
            got = self.swap(jnp.stack(block(me ^ j, 0, rows)), j)
            gate.append((got, 0, (me ^ j) * rows))
            up.append((got, 1, (me ^ j) * rows))
        return gate, up

    def sum_whole(self, v):
        cur = yield from self.scatter_rows(v)
        for b in range(self.ctxs.bit_length() - 1):
            [got] = yield [self.swap_ctx(cur, 1 << b)], [cur]
            cur = add_low(cur, got)
        return cur

    def scatter(self, pieces):
        pieces = dict(enumerate(pieces))
        for bit in self.bits:
            give = {j: p for j, p in pieces.items() if j & bit}
            got = yield [self.swap(p, bit) for p in give.values()], list(give.values())
            pieces = {j ^ bit: add_low(pieces[j ^ bit], g) for j, g in zip(give, got, strict=True)}
        return pieces[0]

    def scatter_rows(self, v, add=add_low):
        cur = v.reshape(self.shards, v.shape[0] // self.shards, *v.shape[1:])
        for bit in self.bits:
            pairs = cur.reshape(cur.shape[0] // 2, 2, *cur.shape[1:])
            mine = self.my_bit(bit)
            keep = lax.dynamic_index_in_dim(pairs, mine, 1, False)
            give = lax.dynamic_index_in_dim(pairs, 1 - mine, 1, False)
            [got] = yield [self.swap(give, bit)], [give]
            cur = add(keep, got)
        return cur[0]

    def ring_gather(self, v):
        n = self.ctxs
        pieces = {0: v}
        a, b = v, v
        for step in range(1, n // 2 + 1):
            both = n - step > n // 2
            got = yield [self.go_right(a)] + ([self.go_left(b)] if both else []), [a, b] if both else [a]
            pieces[step] = a = got[0]
            if both:
                pieces[n - step] = b = got[1]
        return jnp.stack([pieces[k] for k in range(n)])

    def ring_scatter(self, v):
        n = self.ctxs
        m = n // 2
        a, b = v[m], v[m - 1]
        for step in range(1, m):
            a, b = yield [self.go_right(a), self.go_left(b)], [a, b]
            a = add_low(a, v[m + step])
            if step < m - 1:
                b = add_low(b, v[m - 1 - step])
        [a] = yield [self.go_right(a)], [a]
        return v[0].astype(jnp.float32) + a.astype(jnp.float32) + b.astype(jnp.float32)

    def ring_reduce(self, own, axis):
        m = self.ctxs // 2
        far = own(m)
        cut = far.shape[axis] // 2
        head = functools.partial(lax.slice_in_dim, start_index=0, limit_index=cut, axis=axis)
        tail = functools.partial(lax.slice_in_dim, start_index=cut, limit_index=None, axis=axis)
        a, b = head(far), tail(far)
        for k in range(m - 1, -1, -1):
            a, b = yield [self.go_right(a), self.go_left(b)], [a, b]
            at_a, at_b = own(k), own(-k)
            if k == 0:
                total = at_a.astype(jnp.float32) + a.astype(jnp.float32) + b.astype(jnp.float32)
            elif k == m - 1:
                a = jnp.concatenate([add_low(a, head(at_a)), tail(at_a)], axis)
                b = jnp.concatenate([head(at_b), add_low(b, tail(at_b))], axis)
            else:
                a, b = add_low(a, at_a), add_low(b, at_b)
        return total.astype(jnp.bfloat16)

    def ring_spread(self, out, chunk, col):
        m = self.ctxs // 2
        place = self.my_place()
        cut = chunk.shape[1] // 2

        def put(piece, k, col):
            at = lax.rem(place + k + 2 * m, 2 * m) * piece.shape[0]
            out[0] = lax.dynamic_update_slice(out[0], piece.astype(jnp.float32), (at, col))

        put(chunk, 0, col)
        a = b = chunk
        for k in range(1, m + 1):
            if k == m:
                a, b = a[:, :cut], b[:, cut:]
            a, b = yield [self.go_right(a), self.go_left(b)], [a, b]
            put(a, -k, col)
            put(b, k, col + cut if k == m else col)

    def own_chunk(self, chunks, axis):
        place = self.my_place()
        n = self.ctxs
        return lambda k: lax.dynamic_index_in_dim(chunks, lax.rem(place + k + n, n), axis, False)

    def sum_rows(self, v, out):
        rows, cols = v.shape
        chunks = v.reshape(self.ctxs, rows // self.ctxs, cols)
        mine = yield from self.ring_reduce(self.own_chunk(chunks, 0), 1)
        yield from self.ring_spread(out, mine, 0)
        return out[0]

    def sum_over_all(self, v, out):
        mine = yield from self.scatter_rows(v)
        return (yield from self.sum_rows(mine, out))

    def sum_columns(self, part, out, col):
        n, c = self.shards, self.ctxs
        me = lax.axis_index("shard")
        rows, units = part.shape[0] // n // c, part.shape[1]
        mine = yield from self.ring_reduce(self.own_chunk(part.reshape(n, c, rows, units), 1), 0)
        got = [lax.dynamic_index_in_dim(mine, me ^ j, 0, False) for j in range(n)]
        others = yield [self.swap(g, j) for j, g in enumerate(got) if j], got[1:]
        whole = blank((rows, n * units), jnp.bfloat16)
        for j, g in enumerate([got[0], *others]):
            whole = lax.dynamic_update_slice(whole, g, (0, (me ^ j) * units))
        yield from self.ring_spread(out, whole, col)
        return out[0]


def body(plan, tokens, segments, assign, w_qkv, w_out, w_gate_up, w_down, gain_attn, gain_ffn, cotangent):
    seqs, rows_dev, width = tokens.shape
    rows = seqs * rows_dev
    blocks = assign.shape[0]
    n = plan.shards
    low = jnp.bfloat16
    ids = jnp.arange(blocks, dtype=jnp.int32)
    my_blocks = lax.dynamic_slice_in_dim(assign, 2 * lax.axis_index("ctx"), 2, 0)
    place_of = jnp.array([plan.place[i // 2] for i in range(blocks)], jnp.int32)
    back = lax.rem(plan.my_place() - place_of + plan.ctxs, plan.ctxs)
    hit = assign[None, :] == ids[:, None]
    slot_of = jnp.sum(jnp.where(hit, back[None, :], 0), axis=1)
    half_of = jnp.sum(jnp.where(hit, (ids % 2)[None, :], 0), axis=1)
    firsts = jnp.stack([lax.dynamic_index_in_dim(segments, my_blocks[m] * BLK, 1, False) for m in range(2)], 1)
    starts = jnp.sum((segments[:, None, :] < firsts[:, :, None]).astype(jnp.int32), axis=2)
    lowest = jnp.maximum(jnp.maximum(starts // BLK, my_blocks[None, :] - BACK), 0).reshape(-1)
    scalars = (my_blocks, lowest, slot_of, half_of)
    seg = segments.astype(jnp.float32).reshape(seqs, blocks, 1, BLK)

    order = Order()
    chains = {}

    def chain(steps, name=None):
        chains[name] = Chain(order, steps)
        return chains[name]

    def take(names):
        for name in names:
            chains[name].step()

    first, gains = w_qkv[:, QW:], jnp.stack([gain_attn, gain_ffn])
    first_far, first_near = chain(plan.gather_far(first)), chain(plan.gather_near(first))
    gain_far, gain_near = chain(plan.gather_far(gains)), chain(plan.gather_near(gains))
    tok = tokens.reshape(rows, width).astype(jnp.float32)
    scale_one = inv_rms(tok)
    hat_one = tok * scale_one
    first_far.step()
    gain_far.step()
    q_rows = order.after(w_qkv[:, :QW])
    q_far, q_near = chain(plan.gather_far(q_rows)), chain(plan.gather_near(q_rows))
    kv_rows = first_near.finish() + first_far.finish()
    gains = jnp.zeros((2, width), jnp.float32)
    for j, piece in enumerate(gain_near.finish() + gain_far.finish()):
        at = plan.others()[j] * piece.shape[1]
        gains = lax.dynamic_update_slice(gains, piece.astype(jnp.float32), (0, at))
    gain_one, gain_two = gains
    normed_one = (hat_one * gain_one).astype(low)
    key_value, w_kv = project(normed_one, kv_rows, plan.others(), low)
    key_value = key_value.reshape(seqs, 2, BLK, 2 * HD)
    kv = chain(plan.ring_gather(key_value))
    kv.step()
    grad_low = cotangent.reshape(rows, width)
    gy_near = chain(plan.gather_near(order.after(grad_low)))
    kv.step()
    q_far.step()
    gu = chain(plan.gate_up_columns(order.after(w_gate_up)))
    kv.step()
    w_q = plan.lay_rows(q_near.finish() + q_far.finish())
    queries = dot_f32(normed_one, w_q).astype(low).reshape(seqs, rows_dev, QW)
    order.did(queries)
    kv_all = kv.finish()
    o_rows = order.after(w_out)
    o_far, o_near = chain(plan.gather_far(o_rows)), chain(plan.gather_near(o_rows))
    mixed, lse = attend(scalars, queries, kv_all, seg)
    order.did(mixed)
    gu.step()
    gy_near = gy_near.finish()
    gu.step()
    cuts = [0, rows // 2, rows] if n == 4 else [0, rows]
    parts = [slice(a, b) for a, b in zip(cuts, cuts[1:])]
    gy_far = [chain(plan.gather_far(order.after(grad_low)[parts[0]]))]
    o_far.step()
    o_rows = o_near.finish() + o_far.finish()
    mixed_low = mixed.reshape(rows, QW)
    branch, w_o = project(mixed_low, o_rows, plan.others(), jnp.float32)
    hidden = tok + branch
    order.did(hidden)
    gu = gu.finish()
    gy_far[0].step()
    weights = Weights(*gu, w_down, plan.others())
    scale_two = inv_rms(hidden)
    hat_two = hidden * scale_two
    normed_two = (hat_two * gain_two).astype(low)
    normed_two = order.after(normed_two)
    n2_near = chain(plan.gather_near(normed_two))
    n2_far = [chain(plan.gather_far(normed_two[parts[0]]))]
    for part in parts[1:]:
        gy_far.append(chain(plan.gather_far(order.after(grad_low)[part])))
        n2_far.append(chain(plan.gather_far(order.after(normed_two)[part])))
    held, ends = (), []

    def feed_forward(first, part, n2, gy, ends):
        nonlocal held
        got = []
        for p in range(0, len(n2), 2):
            before = ends[p // 2] if ends else []
            held, end = ffn((first + p) // 2, n, part, n2[p : p + 2], gy[p : p + 2], weights, held, before)
            got.append(end)
        order.did(*[v for end in got for v in end])
        return got

    ends += feed_forward(0, None, n2_near.finish(), gy_near, [])
    far = []
    gy_far[-1].step()
    for i in range(len(parts)):
        n2_far[i].step()
        part = i if len(parts) > 1 else None
        far = feed_forward(n // 2, part, n2_far[i].finish(), gy_far[i].finish(), far)
    ends += far
    d_n2 = [end[i] for end in ends for i in (0, 2)]
    down = [end[i] for end in ends for i in (1, 3)]
    act, d_gate, d_up, n2_all, gy_all = (v.reshape(n * rows, -1) for v in held)

    def grad(left, right):
        part = dot_f32(order.after(left), right, ((0,), (0,))).astype(low)
        order.did(part)
        return part

    def blank_like(w):
        return [blank(w.shape, jnp.float32)]

    chain(plan.scatter(d_n2), "T")
    chain(plan.sum_rows(grad(act, gy_all), blank_like(w_down)), "D")
    take("T")
    out_gate_up = blank_like(w_gate_up)
    chain(plan.sum_columns(grad(n2_all, d_gate), out_gate_up, 0), "G")
    take("D")
    chain(plan.sum_columns(grad(n2_all, d_up), out_gate_up, FF), "U")
    take("GDU")
    d_normed_two = chains["T"].finish().astype(jnp.float32)
    e = d_normed_two * gain_two
    d_hidden = grad_low.astype(jnp.float32) + scale_two * (
        e - hat_two * jnp.mean(e * hat_two, axis=-1, keepdims=True)
    )
    d_branch = d_hidden.astype(low)
    order.did(d_branch)
    chain(plan.scatter(order.after(*down)), "B")
    d_mixed = dot_f32(order.after(d_branch), w_o, ((1,), (1,))).astype(low).reshape(seqs, rows_dev, QW)
    order.did(d_mixed)
    take("GBDU")
    dq, dkv = attend_back(scalars, queries, order.after(d_mixed), mixed, kv_all, seg, lse)
    order.did(dq, dkv)
    chain(plan.ring_scatter(dkv), "K")
    dq = dq.reshape(rows, QW)
    take("DUG")
    chain(plan.sum_over_all(grad(mixed_low, d_branch), blank_like(w_out)), "O")
    out_qkv = blank_like(w_qkv)
    chain(plan.sum_over_all(grad(normed_one, dq), out_qkv), "Q")
    branch = chains["B"].finish().astype(jnp.float32)
    output = (hidden + branch).reshape(seqs, rows_dev, width)
    take("OQKDUGKD")
    dkv_low = chains["K"].finish().astype(low).reshape(rows, 2 * HD)
    part_kv = grad(normed_one, dkv_low)
    take("UDG")
    d_normed_one = dot_f32(dq, w_q, ((1,), (1,))) + dot_f32(order.after(dkv_low), w_kv, ((1,), (1,)))
    gains = jnp.stack([jnp.sum(d_normed_one * hat_one, axis=0), jnp.sum(d_normed_two * hat_two, axis=0)])
    gain_rows = width // n
    more = -(-2 * gain_rows // (32 * HD)) * 16
    gains = jnp.moveaxis(gains.reshape(2, n, gain_rows), 0, 1).reshape(n, 2 * gain_rows).astype(low)
    gains = jnp.pad(gains, ((0, 0), (0, more * 2 * HD - 2 * gain_rows))).reshape(n, more, 2 * HD)
    part_kv = jnp.concatenate([part_kv.reshape(n, gain_rows, 2 * HD), gains], axis=1)
    chain(plan.sum_whole(part_kv.reshape(n * (gain_rows + more), 2 * HD)), "V")
    f = d_normed_one * gain_one
    input_grad = d_hidden + scale_one * (f - hat_one * jnp.mean(f * hat_one, axis=-1, keepdims=True))
    take("VUDQUVQOGQUVOQUVQOVQOQOQGOQOGOGOGO")
    while any(chains[name].running for name in "DGUOQV"):
        take("DGUOQV")
    grad_down, grad_out, grad_gate_up = chains["D"].result, chains["O"].result, out_gate_up[0]
    last = chains["V"].result.astype(jnp.float32)
    grad_qkv = lax.dynamic_update_slice(out_qkv[0], last[:gain_rows], (0, QW))
    grad_gain_attn, grad_gain_ffn = last[gain_rows:].reshape(-1)[: 2 * gain_rows].reshape(2, gain_rows)
    return (
        output,
        input_grad.reshape(seqs, rows_dev, width),
        grad_qkv,
        grad_out,
        grad_gate_up,
        grad_down,
        grad_gain_attn,
        grad_gain_ffn,
    )


def solution(mesh):
    return jax.shard_map(
        functools.partial(body, Plan(mesh)),
        mesh=mesh,
        in_specs=(
            P("shard", "ctx", None),
            P("shard", None),
            P(),
            P("shard", None),
            P("shard", None),
            P("shard", None),
            P("shard", None),
            P("shard"),
            P("shard"),
            P("shard", "ctx", None),
        ),
        out_specs=(
            P("shard", "ctx", None),
            P("shard", "ctx", None),
            P("shard", None),
            P("shard", None),
            P("shard", None),
            P("shard", None),
            P("shard"),
            P("shard"),
        ),
        check_vma=False,
    )
```

```python
import functools

import jax
import jax.numpy as jnp
from jax import lax
from jax.experimental import pallas as pl
from jax.experimental.pallas import tpu as pltpu
from jax.sharding import PartitionSpec as P

H = 12
HD = 128
FF = 4608
W = 1024
BLK = 128
BACK = W // BLK
QW = H * HD

epsilon = 1e-06
masked_score = -1e30
scale = HD ** (-0.5)
log2e = 1.4426950408889634
gelu_c = 0.7978845608028654
gelu_a = 0.044715


def dot_f32(left, right, dims=((1,), (0,))):
    return lax.dot_general(left, right, (dims, ((), ())), preferred_element_type=jnp.float32)


def inv_rms(rows):
    return lax.rsqrt(jnp.mean(rows * rows, axis=-1, keepdims=True) + epsilon)


def add_low(a, b):
    return (a.astype(jnp.float32) + b.astype(jnp.float32)).astype(jnp.bfloat16)


def stack_heads(dst, src):
    for h in range(H):
        dst[h * BLK : (h + 1) * BLK, :] = src[0, :, h * HD : (h + 1) * HD]


def block_bias(seg_ref, seq, q_block, k_block, step):
    q_seg = jnp.broadcast_to(seg_ref[seq, q_block], (BLK, BLK))
    k_seg = jnp.broadcast_to(seg_ref[seq, k_block], (BLK, BLK)).T
    allowed = q_seg == k_seg
    if step in (0, BACK):
        key_at = lax.broadcasted_iota(jnp.int32, (BLK, BLK), 0)
        query_at = lax.broadcasted_iota(jnp.int32, (BLK, BLK), 1)
        allowed &= key_at <= query_at if step == BACK else key_at > query_at
    bias = jnp.where(allowed, 0.0, masked_score)
    return jnp.concatenate([bias] * H, axis=1)


def fold8(v, how):
    return how(v.reshape(BLK // 8, 8, QW), axis=0)


def attend_kernel(
    blk_ref, low_ref, slot_ref, half_ref, q_ref, kv_ref, seg_ref, o_ref, lse_ref, qs, sc, mx, tot, acc
):
    seq, mine = pl.program_id(0), pl.program_id(1)
    q_block = blk_ref[mine]
    lowest = low_ref[seq * 2 + mine]
    stack_heads(qs, q_ref)
    mx[...] = jnp.full(mx.shape, masked_score, jnp.float32)
    tot[...] = jnp.zeros_like(tot)
    acc[...] = jnp.zeros_like(acc)
    for step in range(BACK + 1):
        k_block = q_block - BACK + step

        @pl.when(k_block >= lowest)
        def _(step=step, k_block=k_block):
            keys = kv_ref[slot_ref[k_block], seq, half_ref[k_block], :, :HD]
            s = dot_f32(keys, qs[...], ((1,), (1,))) * (scale * log2e)
            s += block_bias(seg_ref, seq, q_block, k_block, step)
            sc[step * BLK : (step + 1) * BLK, :] = s
            mx[...] = jnp.maximum(mx[...], fold8(s, jnp.max))

    top = jnp.max(mx[...], axis=0, keepdims=True)
    for step in range(BACK + 1):
        k_block = q_block - BACK + step

        @pl.when(k_block >= lowest)
        def _(step=step, k_block=k_block):
            vals = kv_ref[slot_ref[k_block], seq, half_ref[k_block], :, HD:]
            p = jnp.exp2(sc[step * BLK : (step + 1) * BLK, :] - top)
            tot[...] += fold8(p, jnp.sum)
            acc[...] += dot_f32(vals, p.astype(jnp.bfloat16), ((0,), (0,)))

    total = jnp.sum(tot[...], axis=0, keepdims=True)
    out = acc[...] / total
    for h in range(H):
        o_ref[0, :, h * HD : (h + 1) * HD] = out[:, h * BLK : (h + 1) * BLK].T.astype(jnp.bfloat16)
    lse_ref[0, 0] = top + jnp.log2(total)


def attend_back_kernel(
    blk_ref, low_ref, slot_ref, half_ref, q_ref, do_ref, o_ref, kv_ref, seg_ref, lse_ref,
    dq_ref, dkv_ref, qs, dos, dqt, dacc,
):
    seq, mine = pl.program_id(0), pl.program_id(1)
    q_block = blk_ref[mine]
    lowest = low_ref[seq * 2 + mine]

    @pl.when((seq == 0) & (mine == 0))
    def _():
        dacc[...] = jnp.zeros_like(dacc)

    stack_heads(qs, q_ref)
    stack_heads(dos, do_ref)
    dqt[...] = jnp.zeros_like(dqt)
    deltas = []
    for h in range(H):
        cols = slice(h * HD, (h + 1) * HD)
        both = do_ref[0, :, cols].astype(jnp.float32) * o_ref[0, :, cols].astype(jnp.float32)
        deltas.append(jnp.sum(both.T, axis=0, keepdims=True))
    delta = jnp.concatenate(deltas, axis=1)
    lse = lse_ref[0, 0]
    for step in range(BACK + 1):
        k_block = q_block - BACK + step

        @pl.when(k_block >= lowest)
        def _(step=step, k_block=k_block):
            slot, half = slot_ref[k_block], half_ref[k_block]
            keys = kv_ref[slot, seq, half, :, :HD]
            vals = kv_ref[slot, seq, half, :, HD:]
            s = dot_f32(keys, qs[...], ((1,), (1,))) * (scale * log2e)
            p = jnp.exp2(s + block_bias(seg_ref, seq, q_block, k_block, step) - lse)
            dp = dot_f32(vals, dos[...], ((1,), (1,)))
            d_raw = (p * (dp - delta)).astype(jnp.bfloat16)
            dqt[...] += dot_f32(keys, d_raw, ((0,), (0,)))
            dacc[slot, seq, half, :, :HD] += dot_f32(d_raw, qs[...]) * scale
            dacc[slot, seq, half, :, HD:] += dot_f32(p.astype(jnp.bfloat16), dos[...])

    out = dqt[...] * scale
    for h in range(H):
        dq_ref[0, :, h * HD : (h + 1) * HD] = out[:, h * BLK : (h + 1) * BLK].T.astype(jnp.bfloat16)

    @pl.when((seq == pl.num_programs(0) - 1) & (mine == 1))
    def _():
        dkv_ref[...] = dacc[...].astype(jnp.bfloat16)


def whole_spec(shape):
    return pl.BlockSpec(shape, lambda s, m, *_: (0,) * len(shape))


def row_spec():
    return pl.BlockSpec((1, BLK, QW), lambda s, m, *_: (s, m, 0))


lse_spec = pl.BlockSpec((1, 1, 1, QW), lambda s, m, *_: (s, m, 0, 0))
kernel_params = pltpu.CompilerParams(vmem_limit_bytes=48 * 2**20)
small_cost = pl.CostEstimate(flops=2**20, bytes_accessed=2**16, transcendentals=0)


def attend(scalars, qkv, key_value, seg):
    seqs, rows = qkv.shape[:2]
    return pl.pallas_call(
        attend_kernel,
        grid_spec=pltpu.PrefetchScalarGridSpec(
            num_scalar_prefetch=4,
            grid=(seqs, 2),
            in_specs=[row_spec(), whole_spec(key_value.shape), whole_spec(seg.shape)],
            out_specs=[row_spec(), lse_spec],
            scratch_shapes=[
                pltpu.VMEM((QW, HD), jnp.bfloat16),
                pltpu.VMEM((W + BLK, QW), jnp.float32),
                pltpu.VMEM((8, QW), jnp.float32),
                pltpu.VMEM((8, QW), jnp.float32),
                pltpu.VMEM((HD, QW), jnp.float32),
            ],
        ),
        out_shape=[
            jax.ShapeDtypeStruct((seqs, rows, QW), jnp.bfloat16),
            jax.ShapeDtypeStruct((seqs, 2, 1, QW), jnp.float32),
        ],
        compiler_params=kernel_params,
        cost_estimate=small_cost,
        name="attend",
    )(*scalars, qkv, key_value, seg)


def attend_back(scalars, qkv, d_mixed, mixed, key_value, seg, lse):
    seqs, rows = qkv.shape[:2]
    return pl.pallas_call(
        attend_back_kernel,
        grid_spec=pltpu.PrefetchScalarGridSpec(
            num_scalar_prefetch=4,
            grid=(seqs, 2),
            in_specs=[row_spec(), row_spec(), row_spec(), whole_spec(key_value.shape), whole_spec(seg.shape), lse_spec],
            out_specs=[row_spec(), whole_spec(key_value.shape)],
            scratch_shapes=[
                pltpu.VMEM((QW, HD), jnp.bfloat16),
                pltpu.VMEM((QW, HD), jnp.bfloat16),
                pltpu.VMEM((HD, QW), jnp.float32),
                pltpu.VMEM(key_value.shape, jnp.float32),
            ],
        ),
        out_shape=[
            jax.ShapeDtypeStruct((seqs, rows, QW), jnp.bfloat16),
            jax.ShapeDtypeStruct(key_value.shape, jnp.bfloat16),
        ],
        compiler_params=kernel_params,
        cost_estimate=pl.CostEstimate(flops=18 * 10**9, bytes_accessed=12 * 2**20, transcendentals=7 * 10**6),
        name="attend_back",
    )(*scalars, qkv, d_mixed, mixed, key_value, seg, lse)


class Loads:
    def __init__(self, counts, index, at_ref, pieces, stores, sems):
        self.groups, i = [], 0
        for store, count in zip(stores, counts, strict=True):
            group = []
            for _ in range(count):
                at, piece = index[i], pieces[i]
                piece = piece if at is None else piece.at[at]
                rows = piece.shape[0]
                place = store.at[pl.ds(pl.multiple_of(at_ref[i], 16), rows)]
                group.append(pltpu.make_async_copy(piece, place, sems.at[i]))
                i += 1
            self.groups.append(group)

        @pl.when(pl.program_id(0) == 0)
        def _():
            for group in self.groups:
                for copy in group:
                    copy.start()

    def ready(self, i):
        @pl.when(pl.program_id(0) == 0)
        def _():
            for copy in self.groups[i]:
                copy.wait()


def ffn_kernel(counts, index, at_ref, n2_a, gy_a, n2_b, gy_b, *refs):
    *outs, wg_ref, wu_ref, wd_ref, sems = refs[-13:]
    act_ref, dg_ref, du_ref, n2_out, gy_out, dn2_a, down_a, dn2_b, down_b = outs
    loads = Loads(counts, index, at_ref, refs, (wg_ref, wu_ref, wd_ref), sems)
    first = pl.program_id(0) < pl.num_programs(0) // 2
    n2 = jnp.where(first, n2_a[...], n2_b[...])
    gy = jnp.where(first, gy_a[...], gy_b[...])
    n2_out[0] = n2
    gy_out[0] = gy
    loads.ready(0)
    gate = dot_f32(n2, wg_ref[...])
    loads.ready(1)
    up = dot_f32(n2, wu_ref[...])
    loads.ready(2)
    d_act = dot_f32(gy, wd_ref[...], ((1,), (1,)))
    square = gate * gate
    inner = jnp.tanh(gate * (gelu_c + gelu_c * gelu_a * square))
    half = 0.5 + 0.5 * inner
    gelu = gate * half
    slope = half + 0.5 * gate * (1.0 - inner * inner) * (gelu_c + 3.0 * gelu_c * gelu_a * square)
    act = (gelu * up).astype(jnp.bfloat16)
    d_gate = (d_act * up * slope).astype(jnp.bfloat16)
    d_up = (d_act * gelu).astype(jnp.bfloat16)
    act_ref[0] = act
    dg_ref[0] = d_gate
    du_ref[0] = d_up
    dn2 = dot_f32(d_gate, wg_ref[...], ((1,), (1,))) + dot_f32(d_up, wu_ref[...], ((1,), (1,)))
    dn2 = dn2.astype(jnp.bfloat16)
    down = dot_f32(act, wd_ref[...]).astype(jnp.bfloat16)

    @pl.when(first)
    def _():
        dn2_a[...] = dn2
        down_a[...] = down

    @pl.when(jnp.logical_not(first))
    def _():
        dn2_b[...] = dn2
        down_b[...] = down


class Weights:
    def __init__(self, gate, up, w_down, who):
        self.groups = [gate, up, [(w_down, None, 0)]]
        self.counts = list(map(len, self.groups))
        places = [at for group in self.groups for *_, at in group]
        self.places = jnp.concatenate([jnp.stack([jnp.asarray(at, jnp.int32) for at in places]), who])
        self.count = len(places)

    def pieces(self, groups):
        parts = [p for group in self.groups[:groups] for p in group]
        return [p for p, *_ in parts], [i for _, i, _ in parts], self.counts[:groups]


def ffn(pair, pieces, part, n2, gy, weights, held, ends):
    some, width = n2[0].shape
    rows = some if part is None else 2 * some
    arrays, index, counts = weights.pieces(3)
    count, units = len(arrays), arrays[-1].shape[0]
    tile = rows // 2
    steps = 2 if part is None else 1
    at_row = 0 if part is None else part
    held_shapes = [(pieces, rows, units)] * 3 + [(pieces, rows, width)] * 2
    held_spec = [
        pl.BlockSpec((1, tile, s[2]), lambda t, at: (2 * pair + t // steps, at_row + t % steps, 0)) for s in held_shapes
    ]

    def spec(second, first_row):
        def index_map(t, at):
            return (first_row + (jnp.maximum(t - steps, 0) if second else jnp.minimum(t, steps - 1)), 0)

        return pl.BlockSpec((tile, width), index_map)

    kept = [*held, *ends]
    first_out = 0 if held else 5
    out = pl.pallas_call(
        functools.partial(ffn_kernel, counts, index),
        grid_spec=pltpu.PrefetchScalarGridSpec(
            num_scalar_prefetch=1,
            grid=(2 * steps,),
            in_specs=[spec(False, 0)] * 2
            + [spec(True, 0)] * 2
            + [pl.BlockSpec(memory_space=pl.ANY)] * (count + len(kept)),
            out_specs=held_spec + [spec(False, at_row)] * 2 + [spec(True, at_row)] * 2,
            scratch_shapes=[
                pltpu.VMEM((width, units), jnp.bfloat16),
                pltpu.VMEM((width, units), jnp.bfloat16),
                pltpu.VMEM((units, width), jnp.bfloat16),
                pltpu.SemaphoreType.DMA((count,)),
            ],
        ),
        out_shape=[jax.ShapeDtypeStruct(s, jnp.bfloat16) for s in held_shapes]
        + [jax.ShapeDtypeStruct((rows, width), jnp.bfloat16)] * 4,
        input_output_aliases={5 + count + i: first_out + i for i in range(len(kept))},
        compiler_params=pltpu.CompilerParams(vmem_limit_bytes=56 * 2**20),
        cost_estimate=small_cost,
        name="ffn",
    )(weights.places, n2[0], gy[0], n2[1], gy[1], *arrays, *kept)
    return out[:5], out[5:]


def project_kernel(at_ref, x_ref, *refs):
    *pieces, y_ref, w_ref, sems = refs
    copies = []
    for i, piece in enumerate(pieces):
        rows = piece.shape[0]
        place = w_ref.at[pl.ds(pl.multiple_of(at_ref[i] * rows, 16), rows)]
        copies.append(pltpu.make_async_copy(piece, place, sems.at[i]))
    for copy in copies:
        copy.start()
    for copy in copies:
        copy.wait()
    y_ref[...] = dot_f32(x_ref[...], w_ref[...]).astype(y_ref.dtype)


def project(x, pieces, at, dtype):
    rows, cols = pieces[0].shape
    vmem = pl.BlockSpec(memory_space=pltpu.VMEM)
    return pl.pallas_call(
        project_kernel,
        in_specs=[pl.BlockSpec(memory_space=pltpu.SMEM), vmem]
        + [pl.BlockSpec(memory_space=pl.ANY)] * len(pieces),
        out_specs=[vmem, vmem],
        out_shape=[
            jax.ShapeDtypeStruct((x.shape[0], cols), dtype),
            jax.ShapeDtypeStruct((len(pieces) * rows, cols), pieces[0].dtype),
        ],
        scratch_shapes=[pltpu.SemaphoreType.DMA((len(pieces),))],
        compiler_params=kernel_params,
        cost_estimate=small_cost,
        name="project",
    )(at, x, *pieces)


def blank(shape, dtype):
    return pl.pallas_call(
        lambda ref: None,
        out_shape=jax.ShapeDtypeStruct(shape, dtype),
        out_specs=pl.BlockSpec(memory_space=pl.ANY),
        name="blank",
    )()


def tie(v, *after):
    return lax.optimization_barrier((v, *after))[0] if after else v


def blank(shape, dtype):
    return pl.pallas_call(
        lambda ref: None,
        out_shape=jax.ShapeDtypeStruct(shape, dtype),
        out_specs=pl.BlockSpec(memory_space=pl.ANY),
        name="blank",
    )()


def tie(v, *after):
    return lax.optimization_barrier((v, *after))[0] if after else v


class Order:
    def __init__(self):
        self.last = ()

    def after(self, *vals):
        out = lax.optimization_barrier((*vals, *self.last))[: len(vals)] if self.last else vals
        return out[0] if len(vals) == 1 else out

    def did(self, *vals):
        self.last = vals


class Chain:
    def __init__(self, order, steps):
        self.order, self.steps, self.result = order, steps, None
        self.running = True
        self.resume(None)

    def resume(self, taken):
        try:
            self.arriving, sent = self.steps.send(taken)
            self.order.did(*sent)
        except StopIteration as end:
            self.running, self.result = False, end.value
            self.order.did(*jax.tree.leaves(end.value))

    def step(self):
        if self.running:
            taken = self.order.after(*self.arriving)
            self.resume(list(taken) if len(self.arriving) > 1 else [taken])

    def finish(self):
        while self.running:
            self.step()
        return self.result


class Plan:
    def __init__(self, mesh):
        self.shards = mesh.shape["shard"]
        self.ctxs = mesh.shape["ctx"]
        half = self.ctxs // 2
        self.ring = [2 * z for z in range(half)] + [2 * z + 1 for z in reversed(range(half))]
        self.place = [self.ring.index(c) for c in range(self.ctxs)]
        self.right = [(self.ring[i], self.ring[(i + 1) % self.ctxs]) for i in range(self.ctxs)]
        self.left = [(b, a) for a, b in self.right]
        self.bits = [1 << b for b in range(self.shards.bit_length() - 1)]

    def my_place(self):
        table = jnp.array(self.place, jnp.int32)
        at = jnp.arange(self.ctxs, dtype=jnp.int32) == lax.axis_index("ctx")
        return jnp.sum(jnp.where(at, table, 0))

    def swap(self, v, bit):
        return lax.ppermute(v, "shard", [(i, i ^ bit) for i in range(self.shards)])

    def swap_ctx(self, v, bit):
        return lax.ppermute(v, "ctx", [(i, i ^ bit) for i in range(self.ctxs)])

    def go_right(self, v):
        return lax.ppermute(v, "ctx", self.right)

    def go_left(self, v):
        return lax.ppermute(v, "ctx", self.left)

    def my_bit(self, bit):
        return (lax.axis_index("shard") // bit) % 2

    def lay_rows(self, pieces):
        rows, cols = pieces[0].shape
        out = blank((self.shards * rows, cols), pieces[0].dtype)
        for piece, at in zip(pieces, self.others(), strict=True):
            out = lax.dynamic_update_slice(out, piece, (at * rows, 0))
        return out

    def others(self):
        return lax.axis_index("shard") ^ jnp.arange(self.shards, dtype=jnp.int32)

    def near(self, v):
        pieces = {0: v}
        for bit in reversed(self.bits[:-1]):
            pieces |= {j | bit: self.swap(p, bit) for j, p in pieces.items()}
        return [pieces[j] for j in range(self.bits[-1])]

    def gather_near(self, v):
        _, *others = self.near(v)
        return [v, *(yield others, [v])]

    def gather_far(self, v):
        [got] = yield [self.swap(v, self.bits[-1])], [v]
        _, *others = self.near(got)
        return [got, *(yield others, [got])]

    def gather_far_halved(self, v):
        half = v.shape[0] // 2
        y = lax.axis_index("ctx") % 2
        give = lax.dynamic_slice_in_dim(v, y * half, half, 0)
        [mine] = yield [self.swap(give, self.bits[-1])], [give]
        [other] = yield [self.swap_ctx(mine, 1)], [mine]
        whole = blank(v.shape, v.dtype)
        whole = lax.dynamic_update_slice(whole, mine, (y * half, 0))
        whole = lax.dynamic_update_slice(whole, other, ((1 - y) * half, 0))
        _, *others = self.near(whole)
        return [whole, *(yield others, [whole])]

    def gate_up_columns(self, w):
        n = self.shards
        rows, units = w.shape[0], FF // n
        me = lax.axis_index("shard")

        def block(shard, row, count):
            return [lax.dynamic_slice(w, (row, base + shard * units), (count, units)) for base in (0, FF)]

        own = block(me, 0, rows)
        if n == 4 and self.ctxs % 4 == 0:
            y, z = lax.axis_index("ctx") % 2, (lax.axis_index("ctx") // 2) % 2
            half = rows // 2
            pairs = [(c * n + s, c * n + (s ^ 2 ^ (c % 2))) for c in range(self.ctxs) for s in range(n)]
            give = jnp.stack(block(me ^ 2 ^ y, z * half, half))
            [got] = yield [lax.ppermute(give, ("ctx", "shard"), pairs)], [give]
            mine, theirs = (me ^ 2 ^ y) * rows, (me ^ 2 ^ (1 - y)) * rows
            at, far = z * half, (1 - z) * half
            second = [self.swap_ctx(got[0], 1), self.swap_ctx(got[1], 2)]
            near_give = jnp.stack(block(me ^ 1, 0, rows))
            second.append(self.swap(near_give, 1))
            g_y, u_z, near = yield second, [got, near_give]
            give = [jnp.stack([got[0], g_y]), jnp.stack([got[1], u_z])]
            g_z, u_y = yield [self.swap_ctx(give[0], 2), self.swap_ctx(give[1], 1)], give
            gate = [(own[0], None, me * rows), (near, 0, (me ^ 1) * rows), (got, 0, mine + at), (g_y, None, theirs + at)]
            gate += [(g_z, 0, mine + far), (g_z, 1, theirs + far)]
            up = [(own[1], None, me * rows), (near, 1, (me ^ 1) * rows), (got, 1, mine + at), (u_z, None, mine + far)]
            up += [(u_y, 0, theirs + at), (u_y, 1, theirs + far)]
            return gate, up
        gate, up = [(own[0], None, me * rows)], [(own[1], None, me * rows)]
        for j in range(1, n):
            got = self.swap(jnp.stack(block(me ^ j, 0, rows)), j)
            gate.append((got, 0, (me ^ j) * rows))
            up.append((got, 1, (me ^ j) * rows))
        return gate, up

    def sum_whole(self, v):
        cur = yield from self.scatter_rows(v)
        for b in range(self.ctxs.bit_length() - 1):
            [got] = yield [self.swap_ctx(cur, 1 << b)], [cur]
            cur = add_low(cur, got)
        return cur

    def scatter(self, pieces):
        pieces = dict(enumerate(pieces))
        for bit in self.bits:
            give = {j: p for j, p in pieces.items() if j & bit}
            got = yield [self.swap(p, bit) for p in give.values()], list(give.values())
            pieces = {j ^ bit: add_low(pieces[j ^ bit], g) for j, g in zip(give, got, strict=True)}
        return pieces[0]

    def scatter_rows(self, v, add=add_low):
        cur = v.reshape(self.shards, v.shape[0] // self.shards, *v.shape[1:])
        for bit in self.bits:
            pairs = cur.reshape(cur.shape[0] // 2, 2, *cur.shape[1:])
            mine = self.my_bit(bit)
            keep = lax.dynamic_index_in_dim(pairs, mine, 1, False)
            give = lax.dynamic_index_in_dim(pairs, 1 - mine, 1, False)
            [got] = yield [self.swap(give, bit)], [give]
            cur = add(keep, got)
        return cur[0]

    def ring_gather(self, v):
        n = self.ctxs
        pieces = {0: v}
        a, b = v, v
        for step in range(1, n // 2 + 1):
            both = n - step > n // 2
            got = yield [self.go_right(a)] + ([self.go_left(b)] if both else []), [a, b] if both else [a]
            pieces[step] = a = got[0]
            if both:
                pieces[n - step] = b = got[1]
        return jnp.stack([pieces[k] for k in range(n)])

    def ring_scatter(self, v):
        n = self.ctxs
        m = n // 2
        a, b = v[m], v[m - 1]
        for step in range(1, m):
            a, b = yield [self.go_right(a), self.go_left(b)], [a, b]
            a = add_low(a, v[m + step])
            if step < m - 1:
                b = add_low(b, v[m - 1 - step])
        [a] = yield [self.go_right(a)], [a]
        return v[0].astype(jnp.float32) + a.astype(jnp.float32) + b.astype(jnp.float32)

    def ways(self, way):
        return (self.go_right, self.go_left) if way > 0 else (self.go_left, self.go_right)

    def ring_reduce(self, own, way):
        m = self.ctxs // 2
        far, near = self.ways(way)
        a, b = own(way * m), own(-way * (m - 1))
        for k in range(m - 1, 0, -1):
            a, b = yield [far(a), near(b)], [a, b]
            a = add_low(a, own(way * k))
            if k > 1:
                b = add_low(b, own(-way * (k - 1)))
        [a] = yield [far(a)], [a]
        total = own(0).astype(jnp.float32) + a.astype(jnp.float32) + b.astype(jnp.float32)
        return total.astype(jnp.bfloat16)

    def ring_spread(self, out, chunk, col, way):
        m = self.ctxs // 2
        place = self.my_place()
        far, near = self.ways(way)

        def put(piece, k):
            at = lax.rem(place + k + 2 * m, 2 * m) * piece.shape[0]
            out[0] = lax.dynamic_update_slice(out[0], piece.astype(jnp.float32), (at, col))

        put(chunk, 0)
        a = b = chunk
        for k in range(1, m):
            a, b = yield [far(a), near(b)], [a, b]
            put(a, -way * k)
            put(b, way * k)
        [a] = yield [far(a)], [a]
        put(a, m)

    def own_chunk(self, chunks, axis):
        place = self.my_place()
        n = self.ctxs
        return lambda k: lax.dynamic_index_in_dim(chunks, lax.rem(place + k + n, n), axis, False)

    def sum_rows(self, v, out, way):
        rows, cols = v.shape
        chunks = v.reshape(self.ctxs, rows // self.ctxs, cols)
        mine = yield from self.ring_reduce(self.own_chunk(chunks, 0), way)
        yield from self.ring_spread(out, mine, 0, way)
        return out[0]

    def sum_over_all(self, v, out, way):
        mine = yield from self.scatter_rows(v)
        return (yield from self.sum_rows(mine, out, way))

    def sum_columns(self, part, out, col, way):
        n, c = self.shards, self.ctxs
        me = lax.axis_index("shard")
        rows, units = part.shape[0] // n // c, part.shape[1]
        mine = yield from self.ring_reduce(self.own_chunk(part.reshape(n, c, rows, units), 1), way)
        got = [lax.dynamic_index_in_dim(mine, me ^ j, 0, False) for j in range(n)]
        others = yield [self.swap(g, j) for j, g in enumerate(got) if j], got[1:]
        whole = blank((rows, n * units), jnp.bfloat16)
        for j, g in enumerate([got[0], *others]):
            whole = lax.dynamic_update_slice(whole, g, (0, (me ^ j) * units))
        yield from self.ring_spread(out, whole, col, way)
        return out[0]


def body(plan, tokens, segments, assign, w_qkv, w_out, w_gate_up, w_down, gain_attn, gain_ffn, cotangent):
    seqs, rows_dev, width = tokens.shape
    rows = seqs * rows_dev
    blocks = assign.shape[0]
    n = plan.shards
    low = jnp.bfloat16
    ids = jnp.arange(blocks, dtype=jnp.int32)
    my_blocks = lax.dynamic_slice_in_dim(assign, 2 * lax.axis_index("ctx"), 2, 0)
    place_of = jnp.array([plan.place[i // 2] for i in range(blocks)], jnp.int32)
    back = lax.rem(plan.my_place() - place_of + plan.ctxs, plan.ctxs)
    hit = assign[None, :] == ids[:, None]
    slot_of = jnp.sum(jnp.where(hit, back[None, :], 0), axis=1)
    half_of = jnp.sum(jnp.where(hit, (ids % 2)[None, :], 0), axis=1)
    firsts = jnp.stack([lax.dynamic_index_in_dim(segments, my_blocks[m] * BLK, 1, False) for m in range(2)], 1)
    starts = jnp.sum((segments[:, None, :] < firsts[:, :, None]).astype(jnp.int32), axis=2)
    lowest = jnp.maximum(jnp.maximum(starts // BLK, my_blocks[None, :] - BACK), 0).reshape(-1)
    scalars = (my_blocks, lowest, slot_of, half_of)
    seg = segments.astype(jnp.float32).reshape(seqs, blocks, 1, BLK)

    order = Order()
    chains = {}

    def chain(steps, name=None):
        chains[name] = Chain(order, steps)
        return chains[name]

    def take(names):
        for name in names:
            chains[name].step()

    first, gains = w_qkv[:, QW:], jnp.stack([gain_attn, gain_ffn])
    first_far, first_near = chain(plan.gather_far(first)), chain(plan.gather_near(first))
    gain_far, gain_near = chain(plan.gather_far(gains)), chain(plan.gather_near(gains))
    tok = tokens.reshape(rows, width).astype(jnp.float32)
    scale_one = inv_rms(tok)
    hat_one = tok * scale_one
    first_far.step()
    gain_far.step()
    q_rows = order.after(w_qkv[:, :QW])
    q_far, q_near = chain(plan.gather_far(q_rows)), chain(plan.gather_near(q_rows))
    kv_rows = first_near.finish() + first_far.finish()
    gains = jnp.zeros((2, width), jnp.float32)
    for j, piece in enumerate(gain_near.finish() + gain_far.finish()):
        at = plan.others()[j] * piece.shape[1]
        gains = lax.dynamic_update_slice(gains, piece.astype(jnp.float32), (0, at))
    gain_one, gain_two = gains
    normed_one = (hat_one * gain_one).astype(low)
    key_value, w_kv = project(normed_one, kv_rows, plan.others(), low)
    key_value = key_value.reshape(seqs, 2, BLK, 2 * HD)
    kv = chain(plan.ring_gather(key_value))
    kv.step()
    grad_low = cotangent.reshape(rows, width)
    gy_near = chain(plan.gather_near(order.after(grad_low)))
    kv.step()
    q_far.step()
    gu = chain(plan.gate_up_columns(order.after(w_gate_up)))
    kv.step()
    w_q = plan.lay_rows(q_near.finish() + q_far.finish())
    queries = dot_f32(normed_one, w_q).astype(low).reshape(seqs, rows_dev, QW)
    order.did(queries)
    kv_all = kv.finish()
    o_rows = order.after(w_out)
    o_far, o_near = chain(plan.gather_far(o_rows)), chain(plan.gather_near(o_rows))
    mixed, lse = attend(scalars, queries, kv_all, seg)
    order.did(mixed)
    gu.step()
    gy_near = gy_near.finish()
    gu.step()
    cuts = [0, rows // 2, rows] if n == 4 else [0, rows]
    parts = [slice(a, b) for a, b in zip(cuts, cuts[1:])]
    gy_far = [chain(plan.gather_far(order.after(grad_low)[parts[0]]))]
    o_far.step()
    o_rows = o_near.finish() + o_far.finish()
    mixed_low = mixed.reshape(rows, QW)
    branch, w_o = project(mixed_low, o_rows, plan.others(), jnp.float32)
    hidden = tok + branch
    order.did(hidden)
    gu = gu.finish()
    gy_far[0].step()
    weights = Weights(*gu, w_down, plan.others())
    scale_two = inv_rms(hidden)
    hat_two = hidden * scale_two
    normed_two = (hat_two * gain_two).astype(low)
    normed_two = order.after(normed_two)
    n2_near = chain(plan.gather_near(normed_two))
    n2_far = [chain(plan.gather_far(normed_two[parts[0]]))]
    for part in parts[1:]:
        gy_far.append(chain(plan.gather_far(order.after(grad_low)[part])))
        n2_far.append(chain(plan.gather_far(order.after(normed_two)[part])))
    held, ends = (), []

    def feed_forward(first, part, n2, gy, ends):
        nonlocal held
        got = []
        for p in range(0, len(n2), 2):
            before = ends[p // 2] if ends else []
            held, end = ffn((first + p) // 2, n, part, n2[p : p + 2], gy[p : p + 2], weights, held, before)
            got.append(end)
        order.did(*[v for end in got for v in end])
        return got

    ends += feed_forward(0, None, n2_near.finish(), gy_near, [])
    far = []
    gy_far[-1].step()
    for i in range(len(parts)):
        n2_far[i].step()
        part = i if len(parts) > 1 else None
        far = feed_forward(n // 2, part, n2_far[i].finish(), gy_far[i].finish(), far)
    ends += far
    d_n2 = [end[i] for end in ends for i in (0, 2)]
    down = [end[i] for end in ends for i in (1, 3)]
    act, d_gate, d_up, n2_all, gy_all = (v.reshape(n * rows, -1) for v in held)

    def grad(left, right):
        part = dot_f32(order.after(left), right, ((0,), (0,))).astype(low)
        order.did(part)
        return part

    def blank_like(w):
        return [blank(w.shape, jnp.float32)]

    chain(plan.scatter(d_n2), "T")
    chain(plan.sum_rows(grad(act, gy_all), blank_like(w_down), 1), "D")
    take("T")
    out_gate_up = blank_like(w_gate_up)
    chain(plan.sum_columns(grad(n2_all, d_gate), out_gate_up, 0, -1), "G")
    take("D")
    chain(plan.sum_columns(grad(n2_all, d_up), out_gate_up, FF, 1), "U")
    take("GDU")
    d_normed_two = chains["T"].finish().astype(jnp.float32)
    e = d_normed_two * gain_two
    d_hidden = grad_low.astype(jnp.float32) + scale_two * (
        e - hat_two * jnp.mean(e * hat_two, axis=-1, keepdims=True)
    )
    d_branch = d_hidden.astype(low)
    order.did(d_branch)
    chain(plan.scatter(order.after(*down)), "B")
    d_mixed = dot_f32(order.after(d_branch), w_o, ((1,), (1,))).astype(low).reshape(seqs, rows_dev, QW)
    order.did(d_mixed)
    take("GBDU")
    dq, dkv = attend_back(scalars, queries, order.after(d_mixed), mixed, kv_all, seg, lse)
    order.did(dq, dkv)
    chain(plan.ring_scatter(dkv), "K")
    dq = dq.reshape(rows, QW)
    take("DUG")
    chain(plan.sum_over_all(grad(mixed_low, d_branch), blank_like(w_out), -1), "O")
    out_qkv = blank_like(w_qkv)
    chain(plan.sum_over_all(grad(normed_one, dq), out_qkv, 1), "Q")
    branch = chains["B"].finish().astype(jnp.float32)
    output = (hidden + branch).reshape(seqs, rows_dev, width)
    take("OQKDUGKD")
    dkv_low = chains["K"].finish().astype(low).reshape(rows, 2 * HD)
    part_kv = grad(normed_one, dkv_low)
    take("UDG")
    d_normed_one = dot_f32(dq, w_q, ((1,), (1,))) + dot_f32(order.after(dkv_low), w_kv, ((1,), (1,)))
    gains = jnp.stack([jnp.sum(d_normed_one * hat_one, axis=0), jnp.sum(d_normed_two * hat_two, axis=0)])
    gain_rows = width // n
    more = -(-2 * gain_rows // (32 * HD)) * 16
    gains = jnp.moveaxis(gains.reshape(2, n, gain_rows), 0, 1).reshape(n, 2 * gain_rows).astype(low)
    gains = jnp.pad(gains, ((0, 0), (0, more * 2 * HD - 2 * gain_rows))).reshape(n, more, 2 * HD)
    part_kv = jnp.concatenate([part_kv.reshape(n, gain_rows, 2 * HD), gains], axis=1)
    chain(plan.sum_whole(part_kv.reshape(n * (gain_rows + more), 2 * HD)), "V")
    f = d_normed_one * gain_one
    input_grad = d_hidden + scale_one * (f - hat_one * jnp.mean(f * hat_one, axis=-1, keepdims=True))
    take("VUDQUVQOGQUVOQUVQOVQOQOQGOQOGOGOGO")
    while any(chains[name].running for name in "DGUOQV"):
        take("DGUOQV")
    grad_down, grad_out, grad_gate_up = chains["D"].result, chains["O"].result, out_gate_up[0]
    last = chains["V"].result.astype(jnp.float32)
    grad_qkv = lax.dynamic_update_slice(out_qkv[0], last[:gain_rows], (0, QW))
    grad_gain_attn, grad_gain_ffn = last[gain_rows:].reshape(-1)[: 2 * gain_rows].reshape(2, gain_rows)
    return (
        output,
        input_grad.reshape(seqs, rows_dev, width),
        grad_qkv,
        grad_out,
        grad_gate_up,
        grad_down,
        grad_gain_attn,
        grad_gain_ffn,
    )


def solution(mesh):
    return jax.shard_map(
        functools.partial(body, Plan(mesh)),
        mesh=mesh,
        in_specs=(
            P("shard", "ctx", None),
            P("shard", None),
            P(),
            P("shard", None),
            P("shard", None),
            P("shard", None),
            P("shard", None),
            P("shard"),
            P("shard"),
            P("shard", "ctx", None),
        ),
        out_specs=(
            P("shard", "ctx", None),
            P("shard", "ctx", None),
            P("shard", None),
            P("shard", None),
            P("shard", None),
            P("shard", None),
            P("shard"),
            P("shard"),
        ),
        check_vma=False,
    )
```

```python
import functools

import jax
import jax.numpy as jnp
from jax import lax
from jax.experimental import pallas as pl
from jax.experimental.pallas import tpu as pltpu
from jax.sharding import PartitionSpec as P

H = 12
HD = 128
FF = 4608
W = 1024
BLK = 128
BACK = W // BLK
QW = H * HD

epsilon = 1e-06
masked_score = -1e30
scale = HD ** (-0.5)
log2e = 1.4426950408889634
gelu_c = 0.7978845608028654
gelu_a = 0.044715


def dot_f32(left, right, dims=((1,), (0,))):
    return lax.dot_general(left, right, (dims, ((), ())), preferred_element_type=jnp.float32)


def inv_rms(rows):
    return lax.rsqrt(jnp.mean(rows * rows, axis=-1, keepdims=True) + epsilon)


def add_low(a, b):
    return (a.astype(jnp.float32) + b.astype(jnp.float32)).astype(jnp.bfloat16)


def stack_heads(dst, src):
    for h in range(H):
        dst[h * BLK : (h + 1) * BLK, :] = src[0, :, h * HD : (h + 1) * HD]


def block_bias(seg_ref, seq, q_block, k_block, step):
    q_seg = jnp.broadcast_to(seg_ref[seq, q_block], (BLK, BLK))
    k_seg = jnp.broadcast_to(seg_ref[seq, k_block], (BLK, BLK)).T
    allowed = q_seg == k_seg
    if step in (0, BACK):
        key_at = lax.broadcasted_iota(jnp.int32, (BLK, BLK), 0)
        query_at = lax.broadcasted_iota(jnp.int32, (BLK, BLK), 1)
        allowed &= key_at <= query_at if step == BACK else key_at > query_at
    bias = jnp.where(allowed, 0.0, masked_score)
    return jnp.concatenate([bias] * H, axis=1)


def fold8(v, how):
    return how(v.reshape(BLK // 8, 8, QW), axis=0)


def attend_kernel(
    blk_ref, low_ref, slot_ref, half_ref, q_ref, kv_ref, seg_ref, o_ref, lse_ref, qs, sc, mx, tot, acc
):
    seq, mine = pl.program_id(0), pl.program_id(1)
    q_block = blk_ref[mine]
    lowest = low_ref[seq * 2 + mine]
    stack_heads(qs, q_ref)
    mx[...] = jnp.full(mx.shape, masked_score, jnp.float32)
    tot[...] = jnp.zeros_like(tot)
    acc[...] = jnp.zeros_like(acc)
    for step in range(BACK + 1):
        k_block = q_block - BACK + step

        @pl.when(k_block >= lowest)
        def _(step=step, k_block=k_block):
            keys = kv_ref[slot_ref[k_block], seq, half_ref[k_block], :, :HD]
            s = dot_f32(keys, qs[...], ((1,), (1,))) * (scale * log2e)
            s += block_bias(seg_ref, seq, q_block, k_block, step)
            sc[step * BLK : (step + 1) * BLK, :] = s
            mx[...] = jnp.maximum(mx[...], fold8(s, jnp.max))

    top = jnp.max(mx[...], axis=0, keepdims=True)
    for step in range(BACK + 1):
        k_block = q_block - BACK + step

        @pl.when(k_block >= lowest)
        def _(step=step, k_block=k_block):
            vals = kv_ref[slot_ref[k_block], seq, half_ref[k_block], :, HD:]
            p = jnp.exp2(sc[step * BLK : (step + 1) * BLK, :] - top)
            tot[...] += fold8(p, jnp.sum)
            acc[...] += dot_f32(vals, p.astype(jnp.bfloat16), ((0,), (0,)))

    total = jnp.sum(tot[...], axis=0, keepdims=True)
    out = acc[...] / total
    for h in range(H):
        o_ref[0, :, h * HD : (h + 1) * HD] = out[:, h * BLK : (h + 1) * BLK].T.astype(jnp.bfloat16)
    lse_ref[0, 0] = top + jnp.log2(total)


def attend_back_kernel(
    blk_ref, low_ref, slot_ref, half_ref, q_ref, do_ref, o_ref, kv_ref, seg_ref, lse_ref,
    dq_ref, dkv_ref, qs, dos, dqt, dacc,
):
    seq, mine = pl.program_id(0), pl.program_id(1)
    q_block = blk_ref[mine]
    lowest = low_ref[seq * 2 + mine]

    @pl.when((seq == 0) & (mine == 0))
    def _():
        dacc[...] = jnp.zeros_like(dacc)

    stack_heads(qs, q_ref)
    stack_heads(dos, do_ref)
    dqt[...] = jnp.zeros_like(dqt)
    deltas = []
    for h in range(H):
        cols = slice(h * HD, (h + 1) * HD)
        both = do_ref[0, :, cols].astype(jnp.float32) * o_ref[0, :, cols].astype(jnp.float32)
        deltas.append(jnp.sum(both.T, axis=0, keepdims=True))
    delta = jnp.concatenate(deltas, axis=1)
    lse = lse_ref[0, 0]
    for step in range(BACK + 1):
        k_block = q_block - BACK + step

        @pl.when(k_block >= lowest)
        def _(step=step, k_block=k_block):
            slot, half = slot_ref[k_block], half_ref[k_block]
            keys = kv_ref[slot, seq, half, :, :HD]
            vals = kv_ref[slot, seq, half, :, HD:]
            s = dot_f32(keys, qs[...], ((1,), (1,))) * (scale * log2e)
            p = jnp.exp2(s + block_bias(seg_ref, seq, q_block, k_block, step) - lse)
            dp = dot_f32(vals, dos[...], ((1,), (1,)))
            d_raw = (p * (dp - delta)).astype(jnp.bfloat16)
            dqt[...] += dot_f32(keys, d_raw, ((0,), (0,)))
            dacc[slot, seq, half, :, :HD] += dot_f32(d_raw, qs[...]) * scale
            dacc[slot, seq, half, :, HD:] += dot_f32(p.astype(jnp.bfloat16), dos[...])

    out = dqt[...] * scale
    for h in range(H):
        dq_ref[0, :, h * HD : (h + 1) * HD] = out[:, h * BLK : (h + 1) * BLK].T.astype(jnp.bfloat16)

    @pl.when((seq == pl.num_programs(0) - 1) & (mine == 1))
    def _():
        dkv_ref[...] = dacc[...].astype(jnp.bfloat16)


def whole_spec(shape):
    return pl.BlockSpec(shape, lambda s, m, *_: (0,) * len(shape))


def row_spec():
    return pl.BlockSpec((1, BLK, QW), lambda s, m, *_: (s, m, 0))


lse_spec = pl.BlockSpec((1, 1, 1, QW), lambda s, m, *_: (s, m, 0, 0))
kernel_params = pltpu.CompilerParams(vmem_limit_bytes=48 * 2**20)
small_cost = pl.CostEstimate(flops=2**20, bytes_accessed=2**16, transcendentals=0)


def attend(scalars, qkv, key_value, seg):
    seqs, rows = qkv.shape[:2]
    return pl.pallas_call(
        attend_kernel,
        grid_spec=pltpu.PrefetchScalarGridSpec(
            num_scalar_prefetch=4,
            grid=(seqs, 2),
            in_specs=[row_spec(), whole_spec(key_value.shape), whole_spec(seg.shape)],
            out_specs=[row_spec(), lse_spec],
            scratch_shapes=[
                pltpu.VMEM((QW, HD), jnp.bfloat16),
                pltpu.VMEM((W + BLK, QW), jnp.float32),
                pltpu.VMEM((8, QW), jnp.float32),
                pltpu.VMEM((8, QW), jnp.float32),
                pltpu.VMEM((HD, QW), jnp.float32),
            ],
        ),
        out_shape=[
            jax.ShapeDtypeStruct((seqs, rows, QW), jnp.bfloat16),
            jax.ShapeDtypeStruct((seqs, 2, 1, QW), jnp.float32),
        ],
        compiler_params=kernel_params,
        cost_estimate=small_cost,
        name="attend",
    )(*scalars, qkv, key_value, seg)


def attend_back(scalars, qkv, d_mixed, mixed, key_value, seg, lse):
    seqs, rows = qkv.shape[:2]
    return pl.pallas_call(
        attend_back_kernel,
        grid_spec=pltpu.PrefetchScalarGridSpec(
            num_scalar_prefetch=4,
            grid=(seqs, 2),
            in_specs=[row_spec(), row_spec(), row_spec(), whole_spec(key_value.shape), whole_spec(seg.shape), lse_spec],
            out_specs=[row_spec(), whole_spec(key_value.shape)],
            scratch_shapes=[
                pltpu.VMEM((QW, HD), jnp.bfloat16),
                pltpu.VMEM((QW, HD), jnp.bfloat16),
                pltpu.VMEM((HD, QW), jnp.float32),
                pltpu.VMEM(key_value.shape, jnp.float32),
            ],
        ),
        out_shape=[
            jax.ShapeDtypeStruct((seqs, rows, QW), jnp.bfloat16),
            jax.ShapeDtypeStruct(key_value.shape, jnp.bfloat16),
        ],
        compiler_params=kernel_params,
        cost_estimate=pl.CostEstimate(flops=18 * 10**9, bytes_accessed=12 * 2**20, transcendentals=7 * 10**6),
        name="attend_back",
    )(*scalars, qkv, d_mixed, mixed, key_value, seg, lse)


class Loads:
    def __init__(self, counts, index, at_ref, pieces, stores, sems):
        self.groups, i = [], 0
        for store, count in zip(stores, counts, strict=True):
            group = []
            for _ in range(count):
                at, piece = index[i], pieces[i]
                piece = piece if at is None else piece.at[at]
                rows = piece.shape[0]
                place = store.at[pl.ds(pl.multiple_of(at_ref[i], 16), rows)]
                group.append(pltpu.make_async_copy(piece, place, sems.at[i]))
                i += 1
            self.groups.append(group)

        @pl.when(pl.program_id(0) == 0)
        def _():
            for group in self.groups:
                for copy in group:
                    copy.start()

    def ready(self, i):
        @pl.when(pl.program_id(0) == 0)
        def _():
            for copy in self.groups[i]:
                copy.wait()


def ffn_kernel(counts, index, at_ref, n2_a, gy_a, n2_b, gy_b, *refs):
    *outs, wg_ref, wu_ref, wd_ref, sems = refs[-13:]
    act_ref, dg_ref, du_ref, n2_out, gy_out, dn2_a, down_a, dn2_b, down_b = outs
    loads = Loads(counts, index, at_ref, refs, (wg_ref, wu_ref, wd_ref), sems)
    first = pl.program_id(0) < pl.num_programs(0) // 2
    n2 = jnp.where(first, n2_a[...], n2_b[...])
    gy = jnp.where(first, gy_a[...], gy_b[...])
    n2_out[0] = n2
    gy_out[0] = gy
    loads.ready(0)
    gate = dot_f32(n2, wg_ref[...])
    loads.ready(1)
    up = dot_f32(n2, wu_ref[...])
    loads.ready(2)
    d_act = dot_f32(gy, wd_ref[...], ((1,), (1,)))
    square = gate * gate
    inner = jnp.tanh(gate * (gelu_c + gelu_c * gelu_a * square))
    half = 0.5 + 0.5 * inner
    gelu = gate * half
    slope = half + 0.5 * gate * (1.0 - inner * inner) * (gelu_c + 3.0 * gelu_c * gelu_a * square)
    act = (gelu * up).astype(jnp.bfloat16)
    d_gate = (d_act * up * slope).astype(jnp.bfloat16)
    d_up = (d_act * gelu).astype(jnp.bfloat16)
    act_ref[0] = act
    dg_ref[0] = d_gate
    du_ref[0] = d_up
    dn2 = dot_f32(d_gate, wg_ref[...], ((1,), (1,))) + dot_f32(d_up, wu_ref[...], ((1,), (1,)))
    dn2 = dn2.astype(jnp.bfloat16)
    down = dot_f32(act, wd_ref[...]).astype(jnp.bfloat16)

    @pl.when(first)
    def _():
        dn2_a[...] = dn2
        down_a[...] = down

    @pl.when(jnp.logical_not(first))
    def _():
        dn2_b[...] = dn2
        down_b[...] = down


class Weights:
    def __init__(self, gate, up, w_down, who):
        self.groups = [gate, up, [(w_down, None, 0)]]
        self.counts = list(map(len, self.groups))
        places = [at for group in self.groups for *_, at in group]
        self.places = jnp.concatenate([jnp.stack([jnp.asarray(at, jnp.int32) for at in places]), who])
        self.count = len(places)

    def pieces(self, groups):
        parts = [p for group in self.groups[:groups] for p in group]
        return [p for p, *_ in parts], [i for _, i, _ in parts], self.counts[:groups]


def ffn(pair, pieces, part, n2, gy, weights, held, ends):
    some, width = n2[0].shape
    rows = some if part is None else 2 * some
    arrays, index, counts = weights.pieces(3)
    count, units = len(arrays), arrays[-1].shape[0]
    tile = rows // 2
    steps = 2 if part is None else 1
    at_row = 0 if part is None else part
    held_shapes = [(pieces, rows, units)] * 3 + [(pieces, rows, width)] * 2
    held_spec = [
        pl.BlockSpec((1, tile, s[2]), lambda t, at: (2 * pair + t // steps, at_row + t % steps, 0)) for s in held_shapes
    ]

    def spec(second, first_row):
        def index_map(t, at):
            return (first_row + (jnp.maximum(t - steps, 0) if second else jnp.minimum(t, steps - 1)), 0)

        return pl.BlockSpec((tile, width), index_map)

    kept = [*held, *ends]
    first_out = 0 if held else 5
    out = pl.pallas_call(
        functools.partial(ffn_kernel, counts, index),
        grid_spec=pltpu.PrefetchScalarGridSpec(
            num_scalar_prefetch=1,
            grid=(2 * steps,),
            in_specs=[spec(False, 0)] * 2
            + [spec(True, 0)] * 2
            + [pl.BlockSpec(memory_space=pl.ANY)] * (count + len(kept)),
            out_specs=held_spec + [spec(False, at_row)] * 2 + [spec(True, at_row)] * 2,
            scratch_shapes=[
                pltpu.VMEM((width, units), jnp.bfloat16),
                pltpu.VMEM((width, units), jnp.bfloat16),
                pltpu.VMEM((units, width), jnp.bfloat16),
                pltpu.SemaphoreType.DMA((count,)),
            ],
        ),
        out_shape=[jax.ShapeDtypeStruct(s, jnp.bfloat16) for s in held_shapes]
        + [jax.ShapeDtypeStruct((rows, width), jnp.bfloat16)] * 4,
        input_output_aliases={5 + count + i: first_out + i for i in range(len(kept))},
        compiler_params=pltpu.CompilerParams(vmem_limit_bytes=56 * 2**20),
        cost_estimate=small_cost,
        name="ffn",
    )(weights.places, n2[0], gy[0], n2[1], gy[1], *arrays, *kept)
    return out[:5], out[5:]


def project_kernel(at_ref, x_ref, *refs):
    *pieces, y_ref, w_ref, sems = refs
    copies = []
    for i, piece in enumerate(pieces):
        rows = piece.shape[0]
        place = w_ref.at[pl.ds(pl.multiple_of(at_ref[i] * rows, 16), rows)]
        copies.append(pltpu.make_async_copy(piece, place, sems.at[i]))
    for copy in copies:
        copy.start()
    for copy in copies:
        copy.wait()
    y_ref[...] = dot_f32(x_ref[...], w_ref[...]).astype(y_ref.dtype)


def project(x, pieces, at, dtype):
    rows, cols = pieces[0].shape
    vmem = pl.BlockSpec(memory_space=pltpu.VMEM)
    return pl.pallas_call(
        project_kernel,
        in_specs=[pl.BlockSpec(memory_space=pltpu.SMEM), vmem]
        + [pl.BlockSpec(memory_space=pl.ANY)] * len(pieces),
        out_specs=[vmem, vmem],
        out_shape=[
            jax.ShapeDtypeStruct((x.shape[0], cols), dtype),
            jax.ShapeDtypeStruct((len(pieces) * rows, cols), pieces[0].dtype),
        ],
        scratch_shapes=[pltpu.SemaphoreType.DMA((len(pieces),))],
        compiler_params=kernel_params,
        cost_estimate=small_cost,
        name="project",
    )(at, x, *pieces)


def blank(shape, dtype):
    return pl.pallas_call(
        lambda ref: None,
        out_shape=jax.ShapeDtypeStruct(shape, dtype),
        out_specs=pl.BlockSpec(memory_space=pl.ANY),
        name="blank",
    )()


def tie(v, *after):
    return lax.optimization_barrier((v, *after))[0] if after else v


def blank(shape, dtype):
    return pl.pallas_call(
        lambda ref: None,
        out_shape=jax.ShapeDtypeStruct(shape, dtype),
        out_specs=pl.BlockSpec(memory_space=pl.ANY),
        name="blank",
    )()


def tie(v, *after):
    return lax.optimization_barrier((v, *after))[0] if after else v


class Order:
    def __init__(self):
        self.last = ()

    def after(self, *vals):
        out = lax.optimization_barrier((*vals, *self.last))[: len(vals)] if self.last else vals
        return out[0] if len(vals) == 1 else out

    def did(self, *vals):
        self.last = vals


class Chain:
    def __init__(self, order, steps):
        self.order, self.steps, self.result = order, steps, None
        self.running = True
        self.resume(None)

    def resume(self, taken):
        try:
            self.arriving, sent = self.steps.send(taken)
            self.order.did(*sent)
        except StopIteration as end:
            self.running, self.result = False, end.value
            self.order.did(*jax.tree.leaves(end.value))

    def step(self):
        if self.running:
            taken = self.order.after(*self.arriving)
            self.resume(list(taken) if len(self.arriving) > 1 else [taken])

    def finish(self):
        while self.running:
            self.step()
        return self.result


class Plan:
    def __init__(self, mesh):
        self.shards = mesh.shape["shard"]
        self.ctxs = mesh.shape["ctx"]
        half = self.ctxs // 2
        self.ring = [2 * z for z in range(half)] + [2 * z + 1 for z in reversed(range(half))]
        self.place = [self.ring.index(c) for c in range(self.ctxs)]
        self.right = [(self.ring[i], self.ring[(i + 1) % self.ctxs]) for i in range(self.ctxs)]
        self.left = [(b, a) for a, b in self.right]
        self.bits = [1 << b for b in range(self.shards.bit_length() - 1)]

    def my_place(self):
        table = jnp.array(self.place, jnp.int32)
        at = jnp.arange(self.ctxs, dtype=jnp.int32) == lax.axis_index("ctx")
        return jnp.sum(jnp.where(at, table, 0))

    def swap(self, v, bit):
        return lax.ppermute(v, "shard", [(i, i ^ bit) for i in range(self.shards)])

    def swap_ctx(self, v, bit):
        return lax.ppermute(v, "ctx", [(i, i ^ bit) for i in range(self.ctxs)])

    def go_right(self, v):
        return lax.ppermute(v, "ctx", self.right)

    def go_left(self, v):
        return lax.ppermute(v, "ctx", self.left)

    def my_bit(self, bit):
        return (lax.axis_index("shard") // bit) % 2

    def lay_rows(self, pieces):
        rows, cols = pieces[0].shape
        out = blank((self.shards * rows, cols), pieces[0].dtype)
        for piece, at in zip(pieces, self.others(), strict=True):
            out = lax.dynamic_update_slice(out, piece, (at * rows, 0))
        return out

    def others(self):
        return lax.axis_index("shard") ^ jnp.arange(self.shards, dtype=jnp.int32)

    def near(self, v):
        pieces = {0: v}
        for bit in reversed(self.bits[:-1]):
            pieces |= {j | bit: self.swap(p, bit) for j, p in pieces.items()}
        return [pieces[j] for j in range(self.bits[-1])]

    def gather_near(self, v):
        _, *others = self.near(v)
        return [v, *(yield others, [v])]

    def gather_far(self, v):
        [got] = yield [self.swap(v, self.bits[-1])], [v]
        _, *others = self.near(got)
        return [got, *(yield others, [got])]

    def gather_far_halved(self, v):
        half = v.shape[0] // 2
        y = lax.axis_index("ctx") % 2
        give = lax.dynamic_slice_in_dim(v, y * half, half, 0)
        [mine] = yield [self.swap(give, self.bits[-1])], [give]
        [other] = yield [self.swap_ctx(mine, 1)], [mine]
        whole = blank(v.shape, v.dtype)
        whole = lax.dynamic_update_slice(whole, mine, (y * half, 0))
        whole = lax.dynamic_update_slice(whole, other, ((1 - y) * half, 0))
        _, *others = self.near(whole)
        return [whole, *(yield others, [whole])]

    def gate_up_columns(self, w):
        n = self.shards
        rows, units = w.shape[0], FF // n
        me = lax.axis_index("shard")

        def block(shard, row, count):
            return [lax.dynamic_slice(w, (row, base + shard * units), (count, units)) for base in (0, FF)]

        own = block(me, 0, rows)
        if n == 4 and self.ctxs % 4 == 0:
            y, z = lax.axis_index("ctx") % 2, (lax.axis_index("ctx") // 2) % 2
            half = rows // 2
            pairs = [(c * n + s, c * n + (s ^ 2 ^ (c % 2))) for c in range(self.ctxs) for s in range(n)]
            give = jnp.stack(block(me ^ 2 ^ y, z * half, half))
            [got] = yield [lax.ppermute(give, ("ctx", "shard"), pairs)], [give]
            mine, theirs = (me ^ 2 ^ y) * rows, (me ^ 2 ^ (1 - y)) * rows
            at, far = z * half, (1 - z) * half
            second = [self.swap_ctx(got[0], 1), self.swap_ctx(got[1], 2)]
            near_give = jnp.stack(block(me ^ 1, 0, rows))
            second.append(self.swap(near_give, 1))
            g_y, u_z, near = yield second, [got, near_give]
            give = [jnp.stack([got[0], g_y]), jnp.stack([got[1], u_z])]
            g_z, u_y = yield [self.swap_ctx(give[0], 2), self.swap_ctx(give[1], 1)], give
            gate = [(own[0], None, me * rows), (near, 0, (me ^ 1) * rows), (got, 0, mine + at), (g_y, None, theirs + at)]
            gate += [(g_z, 0, mine + far), (g_z, 1, theirs + far)]
            up = [(own[1], None, me * rows), (near, 1, (me ^ 1) * rows), (got, 1, mine + at), (u_z, None, mine + far)]
            up += [(u_y, 0, theirs + at), (u_y, 1, theirs + far)]
            return gate, up
        gate, up = [(own[0], None, me * rows)], [(own[1], None, me * rows)]
        for j in range(1, n):
            got = self.swap(jnp.stack(block(me ^ j, 0, rows)), j)
            gate.append((got, 0, (me ^ j) * rows))
            up.append((got, 1, (me ^ j) * rows))
        return gate, up

    def sum_whole(self, v):
        cur = yield from self.scatter_rows(v)
        for b in range(self.ctxs.bit_length() - 1):
            [got] = yield [self.swap_ctx(cur, 1 << b)], [cur]
            cur = add_low(cur, got)
        return cur

    def scatter(self, pieces):
        pieces = dict(enumerate(pieces))
        for bit in self.bits:
            give = {j: p for j, p in pieces.items() if j & bit}
            got = yield [self.swap(p, bit) for p in give.values()], list(give.values())
            pieces = {j ^ bit: add_low(pieces[j ^ bit], g) for j, g in zip(give, got, strict=True)}
        return pieces[0]

    def scatter_rows(self, v, add=add_low):
        cur = v.reshape(self.shards, v.shape[0] // self.shards, *v.shape[1:])
        for bit in self.bits:
            pairs = cur.reshape(cur.shape[0] // 2, 2, *cur.shape[1:])
            mine = self.my_bit(bit)
            keep = lax.dynamic_index_in_dim(pairs, mine, 1, False)
            give = lax.dynamic_index_in_dim(pairs, 1 - mine, 1, False)
            [got] = yield [self.swap(give, bit)], [give]
            cur = add(keep, got)
        return cur[0]

    def ring_gather(self, v):
        n = self.ctxs
        pieces = {0: v}
        a, b = v, v
        for step in range(1, n // 2 + 1):
            both = n - step > n // 2
            got = yield [self.go_right(a)] + ([self.go_left(b)] if both else []), [a, b] if both else [a]
            pieces[step] = a = got[0]
            if both:
                pieces[n - step] = b = got[1]
        return jnp.stack([pieces[k] for k in range(n)])

    def ring_scatter(self, v):
        n = self.ctxs
        m = n // 2
        a, b = v[m], v[m - 1]
        for step in range(1, m):
            a, b = yield [self.go_right(a), self.go_left(b)], [a, b]
            a = add_low(a, v[m + step])
            if step < m - 1:
                b = add_low(b, v[m - 1 - step])
        [a] = yield [self.go_right(a)], [a]
        return v[0].astype(jnp.float32) + a.astype(jnp.float32) + b.astype(jnp.float32)

    def ways(self, way):
        return (self.go_right, self.go_left) if way > 0 else (self.go_left, self.go_right)

    def ring_reduce(self, own, way):
        m = self.ctxs // 2
        far, near = self.ways(way)
        a, b = own(way * m), own(-way * (m - 1))
        for k in range(m - 1, 0, -1):
            a, b = yield [far(a), near(b)], [a, b]
            a = add_low(a, own(way * k))
            if k > 1:
                b = add_low(b, own(-way * (k - 1)))
        [a] = yield [far(a)], [a]
        total = own(0).astype(jnp.float32) + a.astype(jnp.float32) + b.astype(jnp.float32)
        return total.astype(jnp.bfloat16)

    def ring_spread(self, out, chunk, col, way):
        m = self.ctxs // 2
        place = self.my_place()
        far, near = self.ways(way)

        def put(piece, k):
            at = lax.rem(place + k + 2 * m, 2 * m) * piece.shape[0]
            out[0] = lax.dynamic_update_slice(out[0], piece.astype(jnp.float32), (at, col))

        put(chunk, 0)
        a = b = chunk
        for k in range(1, m):
            a, b = yield [far(a), near(b)], [a, b]
            put(a, -way * k)
            put(b, way * k)
        [a] = yield [far(a)], [a]
        put(a, m)

    def own_chunk(self, chunks, axis):
        place = self.my_place()
        n = self.ctxs
        return lambda k: lax.dynamic_index_in_dim(chunks, lax.rem(place + k + n, n), axis, False)

    def sum_rows(self, v, out, way):
        rows, cols = v.shape
        chunks = v.reshape(self.ctxs, rows // self.ctxs, cols)
        mine = yield from self.ring_reduce(self.own_chunk(chunks, 0), way)
        yield from self.ring_spread(out, mine, 0, way)
        return out[0]

    def sum_over_all(self, v, out, way):
        mine = yield from self.scatter_rows(v)
        return (yield from self.sum_rows(mine, out, way))

    def sum_columns(self, part, out, col, way):
        n, c = self.shards, self.ctxs
        me = lax.axis_index("shard")
        rows, units = part.shape[0] // n // c, part.shape[1]
        mine = yield from self.ring_reduce(self.own_chunk(part.reshape(n, c, rows, units), 1), way)
        got = [lax.dynamic_index_in_dim(mine, me ^ j, 0, False) for j in range(n)]
        others = yield [self.swap(g, j) for j, g in enumerate(got) if j], got[1:]
        whole = blank((rows, n * units), jnp.bfloat16)
        for j, g in enumerate([got[0], *others]):
            whole = lax.dynamic_update_slice(whole, g, (0, (me ^ j) * units))
        yield from self.ring_spread(out, whole, col, way)
        return out[0]


def body(plan, tokens, segments, assign, w_qkv, w_out, w_gate_up, w_down, gain_attn, gain_ffn, cotangent):
    seqs, rows_dev, width = tokens.shape
    rows = seqs * rows_dev
    blocks = assign.shape[0]
    n = plan.shards
    low = jnp.bfloat16
    ids = jnp.arange(blocks, dtype=jnp.int32)
    my_blocks = lax.dynamic_slice_in_dim(assign, 2 * lax.axis_index("ctx"), 2, 0)
    place_of = jnp.array([plan.place[i // 2] for i in range(blocks)], jnp.int32)
    back = lax.rem(plan.my_place() - place_of + plan.ctxs, plan.ctxs)
    hit = assign[None, :] == ids[:, None]
    slot_of = jnp.sum(jnp.where(hit, back[None, :], 0), axis=1)
    half_of = jnp.sum(jnp.where(hit, (ids % 2)[None, :], 0), axis=1)
    firsts = jnp.stack([lax.dynamic_index_in_dim(segments, my_blocks[m] * BLK, 1, False) for m in range(2)], 1)
    starts = jnp.sum((segments[:, None, :] < firsts[:, :, None]).astype(jnp.int32), axis=2)
    lowest = jnp.maximum(jnp.maximum(starts // BLK, my_blocks[None, :] - BACK), 0).reshape(-1)
    scalars = (my_blocks, lowest, slot_of, half_of)
    seg = segments.astype(jnp.float32).reshape(seqs, blocks, 1, BLK)

    order = Order()
    chains = {}

    def chain(steps, name=None):
        chains[name] = Chain(order, steps)
        return chains[name]

    def take(names):
        for name in names:
            chains[name].step()

    first, gains = w_qkv[:, QW:], jnp.stack([gain_attn, gain_ffn])
    first_far, first_near = chain(plan.gather_far(first)), chain(plan.gather_near(first))
    gain_far, gain_near = chain(plan.gather_far(gains)), chain(plan.gather_near(gains))
    tok = tokens.reshape(rows, width).astype(jnp.float32)
    scale_one = inv_rms(tok)
    hat_one = tok * scale_one
    first_far.step()
    gain_far.step()
    q_rows = order.after(w_qkv[:, :QW])
    q_far, q_near = chain(plan.gather_far(q_rows)), chain(plan.gather_near(q_rows))
    kv_rows = first_near.finish() + first_far.finish()
    gains = jnp.zeros((2, width), jnp.float32)
    for j, piece in enumerate(gain_near.finish() + gain_far.finish()):
        at = plan.others()[j] * piece.shape[1]
        gains = lax.dynamic_update_slice(gains, piece.astype(jnp.float32), (0, at))
    gain_one, gain_two = gains
    normed_one = (hat_one * gain_one).astype(low)
    key_value, w_kv = project(normed_one, kv_rows, plan.others(), low)
    key_value = key_value.reshape(seqs, 2, BLK, 2 * HD)
    kv = chain(plan.ring_gather(key_value))
    kv.step()
    grad_low = cotangent.reshape(rows, width)
    gy_near = chain(plan.gather_near(order.after(grad_low)))
    kv.step()
    q_far.step()
    gu = chain(plan.gate_up_columns(order.after(w_gate_up)))
    kv.step()
    w_q = plan.lay_rows(q_near.finish() + q_far.finish())
    queries = dot_f32(normed_one, w_q).astype(low).reshape(seqs, rows_dev, QW)
    order.did(queries)
    kv_all = kv.finish()
    o_rows = order.after(w_out)
    o_far, o_near = chain(plan.gather_far(o_rows)), chain(plan.gather_near(o_rows))
    mixed, lse = attend(scalars, queries, kv_all, seg)
    order.did(mixed)
    gu.step()
    gy_near = gy_near.finish()
    gu.step()
    cuts = [0, rows // 2, rows] if n == 4 else [0, rows]
    parts = [slice(a, b) for a, b in zip(cuts, cuts[1:])]
    gy_far = [chain(plan.gather_far(order.after(grad_low)[parts[0]]))]
    o_far.step()
    o_rows = o_near.finish() + o_far.finish()
    mixed_low = mixed.reshape(rows, QW)
    branch, w_o = project(mixed_low, o_rows, plan.others(), jnp.float32)
    hidden = tok + branch
    order.did(hidden)
    gu = gu.finish()
    gy_far[0].step()
    weights = Weights(*gu, w_down, plan.others())
    scale_two = inv_rms(hidden)
    hat_two = hidden * scale_two
    normed_two = (hat_two * gain_two).astype(low)
    normed_two = order.after(normed_two)
    n2_near = chain(plan.gather_near(normed_two))
    n2_far = [chain(plan.gather_far(normed_two[parts[0]]))]
    for part in parts[1:]:
        gy_far.append(chain(plan.gather_far(order.after(grad_low)[part])))
        n2_far.append(chain(plan.gather_far(order.after(normed_two)[part])))
    held, ends = (), []

    def feed_forward(first, part, n2, gy, ends):
        nonlocal held
        got = []
        for p in range(0, len(n2), 2):
            before = ends[p // 2] if ends else []
            held, end = ffn((first + p) // 2, n, part, n2[p : p + 2], gy[p : p + 2], weights, held, before)
            got.append(end)
        order.did(*[v for end in got for v in end])
        return got

    ends += feed_forward(0, None, n2_near.finish(), gy_near, [])
    far = []
    gy_far[-1].step()
    for i in range(len(parts)):
        n2_far[i].step()
        part = i if len(parts) > 1 else None
        far = feed_forward(n // 2, part, n2_far[i].finish(), gy_far[i].finish(), far)
    ends += far
    d_n2 = [end[i] for end in ends for i in (0, 2)]
    down = [end[i] for end in ends for i in (1, 3)]
    act, d_gate, d_up, n2_all, gy_all = (v.reshape(n * rows, -1) for v in held)

    def grad(left, right):
        part = dot_f32(order.after(left), right, ((0,), (0,))).astype(low)
        order.did(part)
        return part

    def blank_like(w):
        return [blank(w.shape, jnp.float32)]

    chain(plan.scatter(d_n2), "T")
    chain(plan.sum_rows(grad(act, gy_all), blank_like(w_down), 1), "D")
    take("T")
    out_gate_up = blank_like(w_gate_up)
    chain(plan.sum_columns(grad(n2_all, d_gate), out_gate_up, 0, -1), "G")
    take("D")
    chain(plan.sum_columns(grad(n2_all, d_up), out_gate_up, FF, 1), "U")
    take("GDU")
    d_normed_two = chains["T"].finish().astype(jnp.float32)
    e = d_normed_two * gain_two
    d_hidden = grad_low.astype(jnp.float32) + scale_two * (
        e - hat_two * jnp.mean(e * hat_two, axis=-1, keepdims=True)
    )
    d_branch = d_hidden.astype(low)
    order.did(d_branch)
    chain(plan.scatter(order.after(*down)), "B")
    d_mixed = dot_f32(order.after(d_branch), w_o, ((1,), (1,))).astype(low).reshape(seqs, rows_dev, QW)
    order.did(d_mixed)
    take("GB")
    dq, dkv = attend_back(scalars, queries, order.after(d_mixed), mixed, kv_all, seg, lse)
    order.did(dq, dkv)
    chain(plan.ring_scatter(dkv), "K")
    dq = dq.reshape(rows, QW)
    take("DUGDU")
    chain(plan.sum_over_all(grad(mixed_low, d_branch), blank_like(w_out), -1), "O")
    out_qkv = blank_like(w_qkv)
    chain(plan.sum_over_all(grad(normed_one, dq), out_qkv, 1), "Q")
    branch = chains["B"].finish().astype(jnp.float32)
    output = (hidden + branch).reshape(seqs, rows_dev, width)
    take("OQKDUGKD")
    dkv_low = chains["K"].finish().astype(low).reshape(rows, 2 * HD)
    part_kv = grad(normed_one, dkv_low)
    take("UDG")
    d_normed_one = dot_f32(dq, w_q, ((1,), (1,))) + dot_f32(order.after(dkv_low), w_kv, ((1,), (1,)))
    gains = jnp.stack([jnp.sum(d_normed_one * hat_one, axis=0), jnp.sum(d_normed_two * hat_two, axis=0)])
    gain_rows = width // n
    more = -(-2 * gain_rows // (32 * HD)) * 16
    gains = jnp.moveaxis(gains.reshape(2, n, gain_rows), 0, 1).reshape(n, 2 * gain_rows).astype(low)
    gains = jnp.pad(gains, ((0, 0), (0, more * 2 * HD - 2 * gain_rows))).reshape(n, more, 2 * HD)
    part_kv = jnp.concatenate([part_kv.reshape(n, gain_rows, 2 * HD), gains], axis=1)
    chain(plan.sum_whole(part_kv.reshape(n * (gain_rows + more), 2 * HD)), "V")
    f = d_normed_one * gain_one
    input_grad = d_hidden + scale_one * (f - hat_one * jnp.mean(f * hat_one, axis=-1, keepdims=True))
    take("VUDQUVQOGQUVOQUVQOVQOQOQGOQOGOGOGO")
    while any(chains[name].running for name in "DGUOQV"):
        take("DGUOQV")
    grad_down, grad_out, grad_gate_up = chains["D"].result, chains["O"].result, out_gate_up[0]
    last = chains["V"].result.astype(jnp.float32)
    grad_qkv = lax.dynamic_update_slice(out_qkv[0], last[:gain_rows], (0, QW))
    grad_gain_attn, grad_gain_ffn = last[gain_rows:].reshape(-1)[: 2 * gain_rows].reshape(2, gain_rows)
    return (
        output,
        input_grad.reshape(seqs, rows_dev, width),
        grad_qkv,
        grad_out,
        grad_gate_up,
        grad_down,
        grad_gain_attn,
        grad_gain_ffn,
    )


def solution(mesh):
    return jax.shard_map(
        functools.partial(body, Plan(mesh)),
        mesh=mesh,
        in_specs=(
            P("shard", "ctx", None),
            P("shard", None),
            P(),
            P("shard", None),
            P("shard", None),
            P("shard", None),
            P("shard", None),
            P("shard"),
            P("shard"),
            P("shard", "ctx", None),
        ),
        out_specs=(
            P("shard", "ctx", None),
            P("shard", "ctx", None),
            P("shard", None),
            P("shard", None),
            P("shard", None),
            P("shard", None),
            P("shard"),
            P("shard"),
        ),
        check_vma=False,
    )
```
